32 devices in a mesh: layer: 4 (over y, x), latent: 8 (over z, core).
Axes of the slice: x: 2, y: 2, z: 4, core: 2. Of those that a mesh axis runs over, the one named last changes fastest.
Arguments:
- residual: bfloat16 [4, 512, 1792], P('layer', 'latent'), may hold values from -6 to 6
- target: bfloat16 [4, 512, 1792], P('layer', 'latent'), may hold values from -6 to 6
- enc_weight: bfloat16 [4, 1792, 2048], P('layer', None, 'latent'), may hold values from -0.125 to 0.125
- enc_bias: float32 [4, 2048], P('layer', 'latent'), may hold values from -3 to 3
- dec_weight: bfloat16 [4, 4, 2048, 1792], P(None, 'layer', 'latent'), may hold values from -0.1875 to 0.1875
- active: int32 [4, 8, 4], replicated, may hold values from 0 to 7, all different within a row; in each aligned block of 8 rows (0 to 7, 8 to 15, ..., all dimensions but the last counted through in order) at most 6 rows name the same one
Outputs:
- loss: float32 [], replicated
- enc_grad: bfloat16 [4, 1792, 2048], P('layer', None, 'latent')
- bias_grad: float32 [4, 2048], P('layer', 'latent')
- dec_grad: bfloat16 [4, 4, 2048, 1792], P(None, 'layer', 'latent')
The draws below stay inside these ranges and needn't reach their ends.
Inputs may be any that keep to these rules, and one draw needn't show every extreme that they name: `active`: each row lists 4 different blocks of its layer; within one layer no block is listed on more than 6 token tiles, and in every draw some block of some layer is listed on exactly 6.
All inputs are finite; a program needn't handle non-finite values.
Results may differ from the reference program's by a relative error of at most 0.023.
Values may be sent and summed in bfloat16 or wider, within the bound.
A program may use at most 128 MiB of HBM per device.

```python
import math
import jax
import jax.numpy as jnp
import numpy as np
from jax import lax

D = 1792
BLOCK = 256
TILE = 64
NTILE = 8
LAYERS = 4
FEATS = 2048
BLOCKS = 8
ACT = 4
CAP = 6
TOKENS = 512


def block_scale(stream_key, shape, split, least, largest):
    loudness = 1.0
    for dim, shards_of in split:
        heights = jax.random.uniform(jax.random.fold_in(jax.random.fold_in(stream_key, 6), dim), (shards_of,), jnp.float32, least / len(split), largest / len(split))
        loudness = loudness * jnp.repeat(jnp.exp(heights), shape[dim] // shards_of).reshape((-1,) + (1,) * (len(shape) - 1 - dim))
    return loudness


def shared_out(stream_key, own, number, rows, count, top, limit, skew):
    sequence = jax.random.permutation(stream_key, count)
    heavy_load, usual = shares(count, rows * top, limit, skew, True), shares(count, rows * top, limit, skew, False)
    places = jnp.arange(count)

    def named(sizes, rotation):
        used = int((sizes > 0).sum())
        fixed = max(1, used // 4)
        passed = fixed + (places - fixed + rotation * (used - fixed)) % max(1, count - fixed)
        return jnp.zeros((count,), jnp.int32).at[sequence[jnp.where(places < fixed, places, passed)]].set(jnp.asarray(sizes, jnp.int32))

    sizes = jnp.where(number % 4 == 0, named(heavy_load, number // 4), named(usual, number - number // 4 - 1))
    mixed = jax.random.permutation(jax.random.fold_in(own, 3), count)
    donor, taker = mixed[0:count // 2 * 2:2], mixed[1:count // 2 * 2:2]
    margin = jnp.minimum(sizes[donor] - 1, limit - sizes[taker]) // 2
    margin = jnp.where((donor == sequence[0]) | (taker == sequence[0]) | (sizes[taker] == 0), 0, jnp.maximum(margin, 0))
    passed = jax.random.randint(jax.random.fold_in(own, 4), (count // 2,), 0, 1 << 20) % (margin + 1)
    sizes = sizes.at[donor].add(-passed).at[taker].add(passed)
    labels = jnp.searchsorted(jnp.cumsum(sizes), jnp.arange(rows * top), side="right").astype(jnp.int32)
    grid = labels.reshape(top, rows).T
    grid = grid[jax.random.permutation(jax.random.fold_in(own, 1), rows)]
    rotation = jax.random.randint(jax.random.fold_in(own, 2), (rows, 1), 0, top)
    return jnp.take_along_axis(grid, (jnp.arange(top)[None, :] + rotation) % top, axis=1)


def shares(number_of, total, reach, skew, full):
    portions = [(1 << 20) // math.isqrt(grade ** skew) + 1 for grade in range(1, number_of + 1)]
    largest = reach if full else min(reach, max(-(-total // number_of), total * portions[0] // sum(portions)))
    least = 1 if total - largest >= number_of - 1 else 0
    holding, spare = [largest] + [least] * (number_of - 1), total - largest - least * (number_of - 1)
    while spare > 0:
        free = [i for i in range(1, number_of) if holding[i] < largest] or [i for i in range(1, number_of) if holding[i] < reach]
        pool, budget = sum([portions[i] for i in free]), spare
        for i in free:
            extra = min(reach - holding[i], max(1, budget * portions[i] // pool), spare)
            holding[i] = holding[i] + extra
            spare = spare - extra
    return np.array(holding)


def bell_draw(stream_key, shape, deviation, bound, cuts=(), held_as=jnp.bfloat16):
    drawn = jax.random.normal(stream_key, shape, jnp.float32) * deviation
    if len(cuts) > 0:
        drawn = block_scale(stream_key, shape, cuts, -0.22, 0.18) * drawn
    return jnp.clip(drawn, min=-bound, max=bound).astype(held_as)


def setup_inputs(seed: int = 0) -> dict:
    key_list = jax.random.split(jax.random.key(seed), 7)
    residual = bell_draw(key_list[0], (LAYERS, TOKENS, D), 1.0, 6.0, ((0, 4), (1, 8)))
    target = bell_draw(key_list[1], (LAYERS, TOKENS, D), 1.0, 6.0, ((0, 4), (1, 8)))
    enc_weight = bell_draw(key_list[2], (LAYERS, D, FEATS), D ** -0.5, 0.125, ((0, 4), (2, 8)))
    enc_bias = bell_draw(key_list[3], (LAYERS, FEATS), 0.5, 3.0, ((0, 4), (1, 8)), jnp.float32)
    dec_weight = bell_draw(key_list[4], (LAYERS, LAYERS, FEATS, D), (ACT * BLOCK) ** -0.5, 0.1875, ((1, 4), (2, 8)))
    active_keys = jax.random.split(jax.random.fold_in(key_list[5], 1), LAYERS * NTILE // NTILE)
    active_turns = jax.random.permutation(jax.random.fold_in(key_list[5], 3), LAYERS * NTILE // NTILE)
    active = jax.vmap(lambda own, number: shared_out(jax.random.fold_in(key_list[5], 2), own, number, NTILE, BLOCKS, ACT, CAP, 2))(active_keys, active_turns).reshape((LAYERS, NTILE, ACT))
    return {"residual": residual, "target": target, "enc_weight": enc_weight, "enc_bias": enc_bias, "dec_weight": dec_weight, "active": active}


def reference(residual, target, enc_weight, enc_bias, dec_weight, active):
    layers = residual.shape[0]
    width = ACT * BLOCK
    x_tiles = residual.reshape(layers, NTILE, TILE, D)
    goal = target.reshape(layers, NTILE, TILE, D).astype(jnp.float32)
    enc_blocks = enc_weight.reshape(layers, D, BLOCKS, BLOCK)
    bias_blocks = enc_bias.reshape(layers, BLOCKS, BLOCK)
    dec_blocks = dec_weight.reshape(layers, layers, BLOCKS, BLOCK, D)
    preacts = []
    codes = []
    for source in range(layers):
        def encode(inputs, source=source):
            rows, block_ids = inputs
            weight = jnp.take(enc_blocks[source], block_ids, axis=1).reshape(D, width)
            offset = jnp.take(bias_blocks[source], block_ids, axis=0).reshape(width)
            return jnp.dot(rows, weight, preferred_element_type=jnp.float32) + offset
        preact = lax.map(encode, (x_tiles[source], active[source]))
        preacts.append(preact)
        codes.append(jnp.maximum(preact, 0.0).astype(jnp.bfloat16))
    codes_all = jnp.stack(codes)

    def decode(tile):
        outputs = []
        for dest in range(layers):
            total = jnp.zeros((TILE, D), jnp.float32)
            for source in range(dest + 1):
                weight = jnp.take(dec_blocks[source, dest], active[source, tile], axis=0).reshape(width, D)
                total = total + jnp.dot(codes_all[source, tile], weight, preferred_element_type=jnp.float32)
            outputs.append(total)
        return jnp.stack(outputs)

    recon = lax.map(decode, jnp.arange(NTILE, dtype=jnp.int32))
    errors = jnp.transpose(recon, (1, 0, 2, 3)) - goal
    loss = 0.5 * jnp.mean(errors * errors)
    error_bf = errors.astype(jnp.bfloat16)

    dec_rows = []
    for source in range(layers):
        row = []
        for dest in range(layers):
            if dest < source:
                row.append(jnp.zeros((FEATS, D), jnp.bfloat16))
            else:
                def add_tile(carry, tile, source=source, dest=dest):
                    block_ids = active[source, tile]
                    term = lax.dot_general(codes_all[source, tile], error_bf[dest, tile], (((0,), (0,)), ((), ())), preferred_element_type=jnp.float32)
                    return carry.at[block_ids].add(term.reshape(ACT, BLOCK, D)), None
                carry, _ = lax.scan(add_tile, jnp.zeros((BLOCKS, BLOCK, D), jnp.float32), jnp.arange(NTILE, dtype=jnp.int32))
                row.append((carry / TILE).reshape(FEATS, D).astype(jnp.bfloat16))
        dec_rows.append(jnp.stack(row))
    dec_grad = jnp.stack(dec_rows)

    enc_grads = []
    bias_grads = []
    for source in range(layers):
        def back_tile(carry, tile, source=source):
            enc_sum, bias_sum = carry
            block_ids = active[source, tile]
            code_grad = jnp.zeros((TILE, width), jnp.float32)
            for dest in range(source, layers):
                weight = jnp.take(dec_blocks[source, dest], block_ids, axis=0).reshape(width, D)
                code_grad = code_grad + lax.dot_general(error_bf[dest, tile], weight, (((1,), (1,)), ((), ())), preferred_element_type=jnp.float32)
            pre_grad = jnp.where(preacts[source][tile] > 0, code_grad, jnp.zeros_like(code_grad))
            pre_bf = pre_grad.astype(jnp.bfloat16)
            enc_term = lax.dot_general(x_tiles[source, tile], pre_bf, (((0,), (0,)), ((), ())), preferred_element_type=jnp.float32)
            enc_sum = enc_sum.at[:, block_ids].add(enc_term.reshape(D, ACT, BLOCK))
            bias_sum = bias_sum.at[block_ids].add(jnp.sum(pre_grad, axis=0).reshape(ACT, BLOCK))
            return (enc_sum, bias_sum), None
        start = (jnp.zeros((D, BLOCKS, BLOCK), jnp.float32), jnp.zeros((BLOCKS, BLOCK), jnp.float32))
        (enc_sum, bias_sum), _ = lax.scan(back_tile, start, jnp.arange(NTILE, dtype=jnp.int32))
        enc_grads.append((enc_sum / TILE).reshape(D, FEATS).astype(jnp.bfloat16))
        bias_grads.append((bias_sum / TILE).reshape(FEATS))
    return loss, jnp.stack(enc_grads), jnp.stack(bias_grads), dec_grad
```

```python
import functools

import jax
import jax.numpy as jnp
from jax import lax
from jax.experimental import pallas as pl
from jax.experimental.pallas import tpu as pltpu
from jax.sharding import PartitionSpec as P

D = 1792
BLOCK = 256
TILE = 64
NTILE = 8
CAP = 6
CHIPS = NTILE // 2
PAIR = 2 * TILE
TOKENS = NTILE * TILE
LAYERS = 4
CHUNKS = 2
CW = D // CHUNKS
MESH = pl.DeviceIdType.MESH
ORDER = (1, 3, 2)


def fused_kernel(
    res, tgt, enc_w, bias, dec_w, active,
    loss, enc_g, bias_g, dec_g,
    x, xt, we, wd, goal, masked, codes, part, part_in, shares, share_in, err,
    grad, grad_bf, grad_in, dec_v, enc_v, acc, sum_core, sum_chip, sum_layer,
    load_sem, store_sem, x_send, x_recv, xp_send, xp_recv, c_send, c_recv,
    p_send, p_recv, s_send, s_recv, e_send, e_recv, ep_send, ep_recv, g_send, g_recv,
    l_send, l_recv,
):
    layer = lax.axis_index("layer")
    latent = lax.axis_index("latent")
    z = latent // 2
    core = latent % 2
    partner = (layer, 2 * z + 1 - core)

    def chip(k):
        return (layer, 2 * lax.rem(z + k, CHIPS) + core)

    def half(slot):
        return pl.ds(pl.multiple_of(slot * PAIR + core * TILE, TILE), TILE)

    def remote(src, dst, send, recv, device):
        return pltpu.make_async_remote_copy(
            src_ref=src, dst_ref=dst, send_sem=send, recv_sem=recv,
            device_id=device, device_id_type=MESH,
        )

    own_cols = pl.ds(pl.multiple_of(layer * BLOCK, BLOCK), BLOCK)
    loads = [
        pltpu.make_async_copy(res.at[0], x.at[half(0)], load_sem.at[0]),
        pltpu.make_async_copy(enc_w.at[0], we, load_sem.at[1]),
        pltpu.make_async_copy(dec_w.at[:, 0], wd, load_sem.at[2]),
        pltpu.make_async_copy(tgt.at[0], goal, load_sem.at[3]),
    ]
    for load in loads:
        load.start()

    barrier = pltpu.get_barrier_semaphore()
    pl.semaphore_signal(barrier, inc=1, device_id=partner, device_id_type=MESH)
    for k in range(1, CHIPS):
        pl.semaphore_signal(barrier, inc=1, device_id=chip(k), device_id_type=MESH)
    for d in range(1, LAYERS):
        pl.semaphore_signal(
            barrier, inc=1, device_id=(lax.rem(layer + d, LAYERS), latent), device_id_type=MESH
        )
    pl.semaphore_wait(barrier, 1 + CHIPS - 1 + LAYERS - 1)

    x_out = {
        k: remote(res.at[0], x.at[half(k)], x_send.at[k], x_recv.at[k], chip(k)) for k in ORDER
    }
    xp_out = {0: remote(res.at[0], x.at[half(0)], xp_send.at[0], xp_recv.at[0], partner)}
    xp_out[0].start()
    for k in ORDER:
        x_out[k].start()

    for s in range(1, LAYERS):
        @pl.when(s > layer)
        def _(s=s):
            codes[:, s * BLOCK:(s + 1) * BLOCK] = jnp.zeros((TOKENS, BLOCK), jnp.bfloat16)

    def code_copy(q, t):
        block = codes.at[pl.ds(q * PAIR, PAIR), own_cols]
        return remote(block, block, c_send.at[t, q], c_recv.at[layer, q], (t, latent))

    def code_wait(q, s):
        block = codes.at[pl.ds(q * PAIR, PAIR), pl.ds(s * BLOCK, BLOCK)]
        return remote(block, block, c_send.at[s, q], c_recv.at[s, q], (s, latent))

    def encode(q):
        rows = pl.ds(q * PAIR, PAIR)
        pre = jnp.dot(x[rows, :], we[...], preferred_element_type=jnp.float32) + bias[...]
        first = 2 * lax.rem(z + CHIPS - q, CHIPS)
        for c in range(2):
            listed = [active[layer, first + c, a] for a in range(active.shape[2])]
            hit = functools.reduce(jnp.logical_or, [b == latent for b in listed])
            live = jnp.where(hit, 1.0, 0.0).astype(jnp.float32)
            kept = pre[c * TILE:(c + 1) * TILE] * live
            spot = pl.ds(q * PAIR + c * TILE, TILE)
            masked[spot, :] = kept
            codes[spot, own_cols] = jnp.maximum(kept, 0.0).astype(jnp.bfloat16)
        for t in range(1, LAYERS):
            @pl.when(t > layer)
            def _(t=t):
                code_copy(q, t).start()

    def take_x(k):
        x_out[k].wait_recv()
        xp_out[k] = remote(x.at[half(k)], x.at[half(k)], xp_send.at[k], xp_recv.at[k], partner)
        xp_out[k].start()

    loads[0].wait()
    loads[1].wait()
    xp_out[0].wait_recv()
    encode(0)
    take_x(1)
    take_x(3)
    xp_out[1].wait_recv()
    encode(1)
    take_x(2)
    xp_out[3].wait_recv()
    encode(3)
    xp_out[2].wait_recv()
    encode(2)

    loads[2].wait()
    for q in range(CHIPS):
        for s in range(LAYERS - 1):
            @pl.when(s < layer)
            def _(q=q, s=s):
                code_wait(q, s).wait_recv()
    p_out = []
    for j in range(CHUNKS):
        cols = slice(j * CW, (j + 1) * CW)
        full = jnp.dot(
            codes[...], wd[:, :, cols].reshape(LAYERS * BLOCK, CW),
            preferred_element_type=jnp.float32,
        ).astype(jnp.bfloat16)
        for q in range(CHIPS):
            for c in range(2):
                at = q * PAIR + c * TILE
                part[j, c, q] = full[at:at + TILE]
        p_out.append(
            remote(part.at[j, 1 - core], part_in.at[j], p_send.at[j], p_recv.at[j], partner)
        )
        p_out[j].start()
    s_out = {}
    for j in range(CHUNKS):
        p_out[j].wait_recv()
        for k in ORDER:
            own = part[j, core, CHIPS - k].astype(jnp.float32)
            other = part_in[j, CHIPS - k].astype(jnp.float32)
            shares[j, k] = (own + other).astype(jnp.bfloat16)
            s_out[j, k] = remote(
                shares.at[j, k], share_in.at[j, k], s_send.at[j, k], s_recv.at[j, k], chip(k)
            )
            s_out[j, k].start()

    xt[...] = x[...].T

    loads[3].wait()
    e_out, ep_out = {}, {}
    squares = jnp.zeros((8, 128), jnp.float32)
    for j in range(CHUNKS):
        cols = pl.ds(j * CW, CW)
        total = part[j, core, 0].astype(jnp.float32) + part_in[j, 0].astype(jnp.float32)
        for k in ORDER:
            s_out[j, k].wait_recv()
            total = total + share_in[j, k].astype(jnp.float32)
        error = total - goal[:, j * CW:(j + 1) * CW].astype(jnp.float32)
        err[half(0), cols] = error.astype(jnp.bfloat16)
        block = err.at[half(0), cols]
        for k in ORDER:
            e_out[j, k] = remote(
                block, err.at[half(k), cols], e_send.at[j, k], e_recv.at[j, k], chip(k)
            )
            e_out[j, k].start()
        ep_out[j, 0] = remote(block, block, ep_send.at[j, 0], ep_recv.at[j, 0], partner)
        ep_out[j, 0].start()
        square = jnp.sum((error * error).reshape(TILE // 8, 8, CW), axis=0)
        for b in range(CW // 128):
            squares = squares + square[:, b * 128:(b + 1) * 128]

    sum_core[core] = squares
    l_core = remote(sum_core.at[core], sum_core.at[core], l_send.at[0], l_recv.at[0], partner)
    l_core.start()
    l_core.wait_recv()
    sum_chip[z] = sum_core[0] + sum_core[1]
    l_chip = [
        remote(sum_chip.at[z], sum_chip.at[z], l_send.at[k], l_recv.at[k], chip(k))
        for k in range(1, CHIPS)
    ]
    for copy in l_chip:
        copy.start()

    def take_e(k):
        for j in range(CHUNKS):
            e_out[j, k].wait_recv()
            block = err.at[half(k), pl.ds(j * CW, CW)]
            ep_out[j, k] = remote(block, block, ep_send.at[j, k], ep_recv.at[j, k], partner)
            ep_out[j, k].start()

    def grad_copy(h, s):
        rows = pl.ds(h * 2 * PAIR, 2 * PAIR)
        return remote(
            grad_bf.at[rows, pl.ds(s * BLOCK, BLOCK)], grad_in.at[layer, rows],
            g_send.at[s, h], g_recv.at[layer, h], (s, latent),
        )

    def grad_wait(h, t):
        rows = pl.ds(h * 2 * PAIR, 2 * PAIR)
        return remote(
            grad_bf.at[rows, pl.ds(0, BLOCK)], grad_in.at[t, rows],
            g_send.at[t, h], g_recv.at[t, h], (t, latent),
        )

    def code_grad(h):
        rows = pl.ds(h * 2 * PAIR, 2 * PAIR)
        back = lax.dot_general(
            err[rows, :], wd[...].reshape(LAYERS * BLOCK, D),
            (((1,), (1,)), ((), ())), preferred_element_type=jnp.float32,
        )
        grad[rows, :] = back
        grad_bf[rows, :] = back.astype(jnp.bfloat16)
        for s in range(LAYERS - 1):
            @pl.when(s < layer)
            def _(s=s):
                grad_copy(h, s).start()

    take_e(1)
    for copy in l_chip:
        copy.wait_recv()
    sum_layer[layer] = functools.reduce(jnp.add, [sum_chip[i] for i in range(CHIPS)])
    l_layer = [
        remote(
            sum_layer.at[layer], sum_layer.at[layer],
            l_send.at[CHIPS - 1 + d], l_recv.at[CHIPS - 1 + d],
            (lax.rem(layer + d, LAYERS), latent),
        )
        for d in range(1, LAYERS)
    ]
    for copy in l_layer:
        copy.start()
    take_e(3)
    for k in (0, 1):
        for j in range(CHUNKS):
            ep_out[j, k].wait_recv()
    code_grad(0)
    take_e(2)
    for k in (3, 2):
        for j in range(CHUNKS):
            ep_out[j, k].wait_recv()
    code_grad(1)

    stores = []
    for s in range(LAYERS):
        dec_v[s] = (
            lax.dot_general(
                codes[:, s * BLOCK:(s + 1) * BLOCK], err[...],
                (((0,), (0,)), ((), ())), preferred_element_type=jnp.float32,
            ) * (1.0 / TILE)
        ).astype(jnp.bfloat16)
        stores.append(pltpu.make_async_copy(dec_v.at[s], dec_g.at[s, 0], store_sem.at[s]))
        stores[s].start()

    acc[...] = grad[:, own_cols]
    for t in range(1, LAYERS):
        @pl.when(t > layer)
        def _(t=t):
            grad_wait(0, t).wait_recv()
            grad_wait(1, t).wait_recv()
            acc[...] += grad_in[t].astype(jnp.float32)
    pre_grad = jnp.where(masked[...] > 0, acc[...], 0.0)
    bias_g[...] = jnp.sum(pre_grad, axis=0, keepdims=True) * (1.0 / TILE)
    enc_v[...] = (
        jnp.dot(xt[...], pre_grad.astype(jnp.bfloat16), preferred_element_type=jnp.float32)
        * (1.0 / TILE)
    ).astype(jnp.bfloat16)
    stores.append(pltpu.make_async_copy(enc_v, enc_g.at[0], store_sem.at[LAYERS]))
    stores[LAYERS].start()

    for copy in l_layer:
        copy.wait_recv()
    every = functools.reduce(jnp.add, [sum_layer[i] for i in range(LAYERS)])
    loss[...] = jnp.sum(every, keepdims=True) * (0.5 / (LAYERS * TOKENS * D))

    for copies in (x_out, xp_out, s_out, e_out, ep_out):
        for copy in copies.values():
            copy.wait_send()
    for copy in [*p_out, l_core, *l_chip, *l_layer]:
        copy.wait_send()
    for t in range(LAYERS):
        @pl.when(t > layer)
        def _(t=t):
            for q in range(CHIPS):
                code_copy(q, t).wait_send()

        @pl.when(t < layer)
        def _(t=t):
            for h in range(2):
                grad_copy(h, t).wait_send()
    for store in stores:
        store.wait()


def fused(residual, target, enc_weight, enc_bias, dec_weight, active):
    bf, f32 = jnp.bfloat16, jnp.float32
    vmem, dma = pltpu.VMEM, pltpu.SemaphoreType.DMA
    anywhere = pl.BlockSpec(memory_space=pl.ANY)
    in_vmem = pl.BlockSpec(memory_space=pltpu.VMEM)
    loss, enc_grad, bias_grad, dec_grad = pl.pallas_call(
        fused_kernel,
        out_shape=[
            jax.ShapeDtypeStruct((1, 1), f32),
            jax.ShapeDtypeStruct(enc_weight.shape, bf),
            jax.ShapeDtypeStruct(enc_bias.shape, f32),
            jax.ShapeDtypeStruct(dec_weight.shape, bf),
        ],
        in_specs=[
            anywhere, anywhere, anywhere, in_vmem, anywhere,
            pl.BlockSpec(memory_space=pltpu.SMEM),
        ],
        out_specs=[in_vmem, anywhere, in_vmem, anywhere],
        scratch_shapes=[
            vmem((TOKENS, D), bf),
            vmem((D, TOKENS), bf),
            vmem((D, BLOCK), bf),
            vmem((LAYERS, BLOCK, D), bf),
            vmem((TILE, D), bf),
            vmem((TOKENS, BLOCK), f32),
            vmem((TOKENS, LAYERS * BLOCK), bf),
            vmem((CHUNKS, 2, CHIPS, TILE, CW), bf),
            vmem((CHUNKS, CHIPS, TILE, CW), bf),
            vmem((CHUNKS, CHIPS, TILE, CW), bf),
            vmem((CHUNKS, CHIPS, TILE, CW), bf),
            vmem((TOKENS, D), bf),
            vmem((TOKENS, LAYERS * BLOCK), f32),
            vmem((TOKENS, LAYERS * BLOCK), bf),
            vmem((LAYERS, TOKENS, BLOCK), bf),
            vmem((LAYERS, BLOCK, D), bf),
            vmem((D, BLOCK), bf),
            vmem((TOKENS, BLOCK), f32),
            vmem((2, 8, 128), f32),
            vmem((CHIPS, 8, 128), f32),
            vmem((LAYERS, 8, 128), f32),
            dma((4,)),
            dma((LAYERS + 1,)),
            dma((CHIPS,)),
            dma((CHIPS,)),
            dma((CHIPS,)),
            dma((CHIPS,)),
            dma((LAYERS, CHIPS)),
            dma((LAYERS, CHIPS)),
            dma((CHUNKS,)),
            dma((CHUNKS,)),
            dma((CHUNKS, CHIPS)),
            dma((CHUNKS, CHIPS)),
            dma((CHUNKS, CHIPS)),
            dma((CHUNKS, CHIPS)),
            dma((CHUNKS, CHIPS)),
            dma((CHUNKS, CHIPS)),
            dma((LAYERS, 2)),
            dma((LAYERS, 2)),
            dma((CHIPS + LAYERS - 1,)),
            dma((CHIPS + LAYERS - 1,)),
        ],
        compiler_params=pltpu.CompilerParams(
            collective_id=0, has_side_effects=True, vmem_limit_bytes=48 * 2**20
        ),
        cost_estimate=pl.CostEstimate(
            flops=14 * 2 * TOKENS * D * BLOCK, bytes_accessed=10 * 2**20, transcendentals=0
        ),
        name="transcoder_step",
    )(residual, target, enc_weight, enc_bias, dec_weight, active)
    return (loss[0, 0], enc_grad, bias_grad, dec_grad)


def shifted(value, axis, steps):
    count = lax.axis_size(axis)
    leading, last = (max(0, -steps), min(count, count - steps))
    return lax.ppermute(value, axis, [(source, source + steps) for source in range(leading, last)])


def slot_list(active, layer, my_block, slot_count):
    block_ids = lax.dynamic_index_in_dim(active, layer, 0, keepdims=False)
    hit = jnp.any(block_ids == my_block, axis=1).astype(jnp.int32)
    every = jnp.arange(NTILE, dtype=jnp.int32)
    place = jnp.cumsum(hit) - 1
    chosen = (hit[None, :] == 1) & (
        place[None, :] == jnp.arange(slot_count, dtype=jnp.int32)[:, None]
    )
    tile_ids = jnp.sum(jnp.where(chosen, every[None, :], 0), axis=1)
    filled = jnp.sum(chosen.astype(jnp.float32), axis=1)
    return (tile_ids, filled)


def shards(residual, target, enc_weight, enc_bias, dec_weight, active):
    layers = dec_weight.shape[0]
    feat_dev = enc_weight.shape[2]
    layer_index = lax.axis_index("layer")
    my_block = lax.axis_index("latent") * feat_dev // BLOCK
    slot_count = CAP
    slot_rows = slot_count * TILE
    full_inputs = lax.all_gather(residual[0], "latent", axis=0, tiled=True).reshape(NTILE, TILE, D)
    own_tiles, own_filled = slot_list(active, layer_index, my_block, slot_count)
    rows = jnp.take(full_inputs, own_tiles, axis=0).reshape(slot_rows, D)
    preact = jnp.dot(rows, enc_weight[0], preferred_element_type=jnp.float32) + enc_bias[0][None, :]
    live = jnp.repeat(own_filled, TILE)[:, None]
    sparse_codes = (jnp.maximum(preact, 0.0) * live).astype(jnp.bfloat16)
    dec_all = dec_weight[:, 0]

    def take_source(carry, portion, source):
        writes, kept = carry
        usable = (source >= 0) & (source <= layer_index)
        source_idx = jnp.clip(source, 0, layers - 1)
        portion = jnp.where(usable, portion, jnp.zeros_like(portion))
        tile_ids, _ = slot_list(active, source_idx, my_block, slot_count)
        weight = lax.dynamic_index_in_dim(dec_all, source_idx, 0, keepdims=False)
        product = jnp.dot(portion, weight, preferred_element_type=jnp.float32).reshape(
            slot_count, TILE, D
        )
        writes = writes.at[tile_ids].add(product)
        kept = jnp.where(usable, kept.at[source_idx].set(portion), kept)
        return (writes, kept)

    start_state = (
        jnp.zeros((NTILE, TILE, D), jnp.float32),
        jnp.zeros((layers, slot_rows, feat_dev), jnp.bfloat16),
    )
    state = take_source(start_state, sparse_codes, layer_index)
    moving = sparse_codes
    for hop in range(1, layers):
        moving = shifted(moving, "layer", 1)
        state = take_source(state, moving, layer_index - hop)
    writes, kept = state
    recon = lax.psum_scatter(
        writes.reshape(NTILE * TILE, D), "latent", scatter_dimension=0, tiled=True
    )
    errors = recon - target[0].astype(jnp.float32)
    total = lax.psum(jnp.sum(errors * errors), ("layer", "latent"))
    loss = 0.5 * total / (layers * NTILE * TILE * D)
    full_errors = lax.all_gather(errors.astype(jnp.bfloat16), "latent", axis=0, tiled=True).reshape(
        NTILE, TILE, D
    )
    dec_grads = []
    code_grads = []
    for source in range(layers):
        tile_ids, _ = slot_list(active, source, my_block, slot_count)
        error_part = jnp.take(full_errors, tile_ids, axis=0).reshape(slot_rows, D)
        grad = lax.dot_general(
            kept[source], error_part, (((0,), (0,)), ((), ())), preferred_element_type=jnp.float32
        )
        dec_grads.append((grad / TILE).astype(jnp.bfloat16))
        back = lax.dot_general(
            error_part,
            dec_all[source],
            (((1,), (1,)), ((), ())),
            preferred_element_type=jnp.float32,
        )
        code_grads.append(jnp.where(source <= layer_index, back, jnp.zeros_like(back)))
    dec_grad = jnp.stack(dec_grads)[:, None]
    code_grad = jnp.stack(code_grads)
    running = code_grad
    for hop in range(1, layers):
        running = code_grad + shifted(running, "layer", -1)
    mine = lax.dynamic_index_in_dim(running, layer_index, 0, keepdims=False)
    pre_grad = jnp.where(preact > 0, mine, jnp.zeros_like(mine)) * live
    bias_grad = (jnp.sum(pre_grad, axis=0) / TILE)[None]
    enc_term = lax.dot_general(
        rows,
        pre_grad.astype(jnp.bfloat16),
        (((0,), (0,)), ((), ())),
        preferred_element_type=jnp.float32,
    )
    enc_grad = (enc_term / TILE).astype(jnp.bfloat16)[None]
    return (loss, enc_grad, bias_grad, dec_grad)


def solution(mesh):
    in_specs = (
        P("layer", "latent", None),
        P("layer", "latent", None),
        P("layer", None, "latent"),
        P("layer", "latent"),
        P(None, "layer", "latent", None),
        P(),
    )
    out_specs = (
        P(),
        P("layer", None, "latent"),
        P("layer", "latent"),
        P(None, "layer", "latent", None),
    )
    one_tile_each = mesh.shape["latent"] == NTILE and mesh.shape["layer"] == LAYERS
    step = fused if one_tile_each else shards
    return jax.shard_map(step, mesh=mesh, in_specs=in_specs, out_specs=out_specs, check_vma=False)
```

```python
import functools

import jax
import jax.numpy as jnp
from jax import lax
from jax.experimental import pallas as pl
from jax.experimental.pallas import tpu as pltpu
from jax.sharding import PartitionSpec as P

D = 1792
BLOCK = 256
TILE = 64
NTILE = 8
CAP = 6
CHIPS = NTILE // 2
PAIR = 2 * TILE
TOKENS = NTILE * TILE
LAYERS = 4
CHUNKS = 2
CW = D // CHUNKS
MESH = pl.DeviceIdType.MESH
GROUPS = ((0, 2 * PAIR), (2 * PAIR, PAIR), (3 * PAIR, PAIR))


def fused_kernel(
    res, tgt, enc_w, bias, dec_w, active,
    loss, enc_g, bias_g, dec_g,
    x, xt, we, wd, goal, offset, masked, codes, part, part_in, shares, share_in, err,
    grad, grad_bf, grad_in, acc, sum_core, sum_chip, sum_layer,
    load_sem, x_send, x_recv, xp_send, xp_recv, c_send, c_recv,
    p_send, p_recv, s_send, s_recv, e_send, e_recv, ep_send, ep_recv, g_send, g_recv,
    l_send, l_recv,
):
    layer = lax.axis_index("layer")
    latent = lax.axis_index("latent")
    z = latent // 2
    core = latent % 2
    middle = (z * (CHIPS - 1 - z)) // 2
    mates = (z, z + 1 - 2 * (z % 2), (z + 2) % CHIPS, CHIPS - 1 - z)
    partner = (layer, 2 * z + 1 - core)

    def chip(m):
        return (layer, 2 * mates[m] + core)

    def half(slot):
        return pl.ds(pl.multiple_of(slot * PAIR + core * TILE, TILE), TILE)

    def remote(src, dst, send, recv, device):
        return pltpu.make_async_remote_copy(
            src_ref=src, dst_ref=dst, send_sem=send, recv_sem=recv,
            device_id=device, device_id_type=MESH,
        )

    own_cols = pl.ds(pl.multiple_of(layer * BLOCK, BLOCK), BLOCK)
    loads = [
        pltpu.make_async_copy(res.at[0], x.at[half(0)], load_sem.at[0]),
        pltpu.make_async_copy(enc_w.at[0], we, load_sem.at[1]),
        pltpu.make_async_copy(bias, offset, load_sem.at[4]),
        pltpu.make_async_copy(dec_w.at[:, 0], wd, load_sem.at[2]),
        pltpu.make_async_copy(tgt.at[0], goal, load_sem.at[3]),
    ]
    for load in loads:
        load.start()

    barrier = pltpu.get_barrier_semaphore()
    pl.semaphore_signal(barrier, inc=1, device_id=partner, device_id_type=MESH)
    for m in range(1, CHIPS):
        pl.semaphore_signal(barrier, inc=1, device_id=chip(m), device_id_type=MESH)
    for d in range(1, LAYERS):
        pl.semaphore_signal(
            barrier, inc=1, device_id=(lax.rem(layer + d, LAYERS), latent), device_id_type=MESH
        )
    pl.semaphore_wait(barrier, 1 + CHIPS - 1 + LAYERS - 1)

    x_out = {
        m: remote(res.at[0], x.at[half(m)], x_send.at[m], x_recv.at[m], chip(m))
        for m in (1, 2, 3)
    }
    x_far = remote(x.at[half(2)], x.at[half(3)], x_send.at[0], x_recv.at[3], chip(1))
    xp_out = {0: remote(res.at[0], x.at[half(0)], xp_send.at[0], xp_recv.at[0], partner)}
    xp_out[0].start()
    for m in (1, 2):
        x_out[m].start()

    for s in range(1, LAYERS):
        @pl.when(s > layer)
        def _(s=s):
            codes[:, s * BLOCK:(s + 1) * BLOCK] = jnp.zeros((TOKENS, BLOCK), jnp.bfloat16)

    @pl.when(middle == 0)
    def _():
        for j in range(CHUNKS):
            share_in[j, 3] = jnp.zeros((TILE, CW), jnp.bfloat16)

    def code_copy(q, t):
        block = codes.at[pl.ds(q * PAIR, PAIR), own_cols]
        return remote(block, block, c_send.at[t, q], c_recv.at[layer, q], (t, latent))

    def code_wait(q):
        for s in range(LAYERS - 1):
            @pl.when(s < layer)
            def _(s=s):
                block = codes.at[pl.ds(q * PAIR, PAIR), pl.ds(s * BLOCK, BLOCK)]
                remote(
                    block, block, c_send.at[s, q], c_recv.at[s, q], (s, latent)
                ).wait_recv()

    def encode(q):
        rows = pl.ds(q * PAIR, PAIR)
        pre = jnp.dot(x[rows, :], we[...], preferred_element_type=jnp.float32) + offset[...]
        for c in range(2):
            listed = [active[layer, a, 2 * mates[q] + c] for a in range(active.shape[1])]
            hit = functools.reduce(jnp.logical_or, [b == latent for b in listed])
            live = jnp.where(hit, 1.0, 0.0).astype(jnp.float32)
            kept = pre[c * TILE:(c + 1) * TILE] * live
            spot = pl.ds(q * PAIR + c * TILE, TILE)
            masked[spot, :] = kept
            codes[spot, own_cols] = jnp.maximum(kept, 0.0).astype(jnp.bfloat16)
        for t in range(1, LAYERS):
            @pl.when(t > layer)
            def _(t=t):
                code_copy(q, t).start()

    def take_x(m):
        x_out[m].wait_recv()
        xp_out[m] = remote(x.at[half(m)], x.at[half(m)], xp_send.at[m], xp_recv.at[m], partner)
        xp_out[m].start()

    p_out, s_out = {}, {}

    def decode(g, j):
        full = jnp.dot(
            codes[g * 2 * PAIR:(g + 1) * 2 * PAIR, :],
            wd[:, :, j * CW:(j + 1) * CW].reshape(LAYERS * BLOCK, CW),
            preferred_element_type=jnp.float32,
        ).astype(jnp.bfloat16)
        for q in range(2):
            for c in range(2):
                at = q * PAIR + c * TILE
                part[g, j, c, q] = full[at:at + TILE]
        p_out[g, j] = remote(
            part.at[g, j, 1 - core], part_in.at[g, j], p_send.at[g, j], p_recv.at[g, j], partner
        )
        p_out[g, j].start()

    def chip_sum(j, m):
        own = part[m // 2, j, core, m % 2].astype(jnp.float32)
        return own + part_in[m // 2, j, m % 2].astype(jnp.float32)

    def send_share(j, m, slot, device):
        s_out[j, m] = remote(
            shares.at[j, m], share_in.at[j, slot], s_send.at[j, m], s_recv.at[j, slot], device
        )
        s_out[j, m].start()

    def share_wait(j, slot):
        remote(
            shares.at[j, slot], share_in.at[j, slot], s_send.at[j, slot], s_recv.at[j, slot],
            partner,
        ).wait_recv()

    loads[0].wait()
    loads[1].wait()
    loads[2].wait()
    xp_out[0].wait_recv()
    encode(0)
    take_x(1)
    take_x(2)

    @pl.when(middle == 1)
    def _():
        x_far.start()
        x_out[3].start()

    xp_out[1].wait_recv()
    encode(1)
    xp_out[2].wait_recv()
    encode(2)
    loads[3].wait()
    code_wait(0)
    code_wait(1)
    for j in range(CHUNKS):
        decode(0, j)
    take_x(3)
    for j in range(CHUNKS):
        p_out[0, j].wait_recv()
        shares[j, 1] = chip_sum(j, 1).astype(jnp.bfloat16)
        send_share(j, 1, 1, chip(1))
    xp_out[3].wait_recv()
    encode(3)
    code_wait(2)
    code_wait(3)
    for j in range(CHUNKS):
        decode(1, j)
    far = (layer, 2 * (middle * mates[3] + (1 - middle) * mates[1]) + core)
    for j in range(CHUNKS):
        p_out[1, j].wait_recv()
        shares[j, 3] = chip_sum(j, 3).astype(jnp.bfloat16)
        send_share(j, 3, 3 * middle, far)
    for j in range(CHUNKS):
        @pl.when(middle == 0)
        def _(j=j):
            shares[j, 2] = chip_sum(j, 2).astype(jnp.bfloat16)

        @pl.when(middle == 1)
        def _(j=j):
            share_wait(j, 0)
            shares[j, 2] = (
                chip_sum(j, 2) + share_in[j, 0].astype(jnp.float32)
            ).astype(jnp.bfloat16)

        send_share(j, 2, 2, chip(2))

    xt[...] = x[...].T

    loads[4].wait()
    e_out, ep_out, e_far = {}, {}, {}
    squares = jnp.zeros((8, 128), jnp.float32)
    for j in range(CHUNKS):
        cols = pl.ds(j * CW, CW)
        share_wait(j, 1)
        share_wait(j, 2)

        @pl.when(middle == 1)
        def _(j=j):
            share_wait(j, 3)

        total = chip_sum(j, 0)
        for m in (1, 2, 3):
            total = total + share_in[j, m].astype(jnp.float32)
        error = total - goal[:, j * CW:(j + 1) * CW].astype(jnp.float32)
        err[half(0), cols] = error.astype(jnp.bfloat16)
        block = err.at[half(0), cols]
        for m in (1, 2, 3):
            e_out[j, m] = remote(
                block, err.at[half(m), cols], e_send.at[j, m], e_recv.at[j, m], chip(m)
            )
        e_far[j] = remote(
            err.at[half(2), cols], err.at[half(3), cols], e_send.at[j, 0], e_recv.at[j, 3], chip(1)
        )
        for m in (2, 1):
            e_out[j, m].start()
        ep_out[j, 0] = remote(block, block, ep_send.at[j, 0], ep_recv.at[j, 0], partner)
        ep_out[j, 0].start()
        square = jnp.sum((error * error).reshape(TILE // 8, 8, CW), axis=0)
        for b in range(CW // 128):
            squares = squares + square[:, b * 128:(b + 1) * 128]

    sum_core[core] = squares
    l_core = remote(sum_core.at[core], sum_core.at[core], l_send.at[0], l_recv.at[0], partner)
    l_core.start()

    def take_e(j, m):
        e_out[j, m].wait_recv()
        block = err.at[half(m), pl.ds(j * CW, CW)]
        ep_out[j, m] = remote(block, block, ep_send.at[j, m], ep_recv.at[j, m], partner)
        ep_out[j, m].start()

    def grad_copy(i, s):
        rows = pl.ds(*GROUPS[i])
        return remote(
            grad_bf.at[rows, pl.ds(s * BLOCK, BLOCK)], grad_in.at[layer, rows],
            g_send.at[s, i], g_recv.at[layer, i], (s, latent),
        )

    def grad_wait(i, t):
        rows = pl.ds(*GROUPS[i])
        remote(
            grad_bf.at[rows, pl.ds(0, BLOCK)], grad_in.at[t, rows],
            g_send.at[t, i], g_recv.at[t, i], (t, latent),
        ).wait_recv()

    def code_grad(i):
        rows = pl.ds(*GROUPS[i])
        back = lax.dot_general(
            err[rows, :], wd[...].reshape(LAYERS * BLOCK, D),
            (((1,), (1,)), ((), ())), preferred_element_type=jnp.float32,
        )
        grad[rows, :] = back
        grad_bf[rows, :] = back.astype(jnp.bfloat16)
        for s in range(LAYERS - 1):
            @pl.when(s < layer)
            def _(s=s):
                grad_copy(i, s).start()

    for j in range(CHUNKS):
        take_e(j, 2)

        @pl.when(middle == 1)
        def _(j=j):
            e_far[j].start()
            e_out[j, 3].start()

        take_e(j, 1)
    l_core.wait_recv()
    sum_chip[z] = sum_core[0] + sum_core[1]
    l_chip = [
        remote(sum_chip.at[z], sum_chip.at[z], l_send.at[m], l_recv.at[m], chip(m))
        for m in range(1, CHIPS)
    ]
    for copy in l_chip:
        copy.start()
    for m in (0, 1):
        for j in range(CHUNKS):
            ep_out[j, m].wait_recv()
    code_grad(0)
    for j in range(CHUNKS):
        ep_out[j, 2].wait_recv()
    code_grad(1)
    for copy in l_chip:
        copy.wait_recv()
    sum_layer[layer] = functools.reduce(jnp.add, [sum_chip[i] for i in range(CHIPS)])
    l_layer = [
        remote(
            sum_layer.at[layer], sum_layer.at[layer],
            l_send.at[CHIPS - 1 + d], l_recv.at[CHIPS - 1 + d],
            (lax.rem(layer + d, LAYERS), latent),
        )
        for d in range(1, LAYERS)
    ]
    for copy in l_layer:
        copy.start()
    for j in range(CHUNKS):
        take_e(j, 3)
    for j in range(CHUNKS):
        ep_out[j, 3].wait_recv()
    code_grad(2)

    for s in range(LAYERS):
        dec_g[s, 0] = lax.dot_general(
            codes[:, s * BLOCK:(s + 1) * BLOCK], err[...],
            (((0,), (0,)), ((), ())), preferred_element_type=jnp.float32,
        ).astype(jnp.bfloat16)

    acc[...] = grad[:, own_cols]
    for t in range(1, LAYERS):
        @pl.when(t > layer)
        def _(t=t):
            for i in range(len(GROUPS)):
                grad_wait(i, t)
            acc[...] += grad_in[t].astype(jnp.float32)
    pre_grad = jnp.where(masked[...] > 0, acc[...], 0.0)
    bias_g[...] = jnp.sum(pre_grad, axis=0, keepdims=True)
    enc_g[0] = jnp.dot(
        xt[...], pre_grad.astype(jnp.bfloat16), preferred_element_type=jnp.float32
    ).astype(jnp.bfloat16)

    for copy in l_layer:
        copy.wait_recv()
    every = functools.reduce(jnp.add, [sum_layer[i] for i in range(LAYERS)])
    loss[...] = jnp.sum(every, keepdims=True)

    for m in (1, 2):
        x_out[m].wait_send()
        for j in range(CHUNKS):
            e_out[j, m].wait_send()

    @pl.when(middle == 1)
    def _():
        for copy in [x_far, x_out[3], *e_far.values(), *[e_out[j, 3] for j in range(CHUNKS)]]:
            copy.wait_send()

    for copies in (xp_out, p_out, s_out, ep_out):
        for copy in copies.values():
            copy.wait_send()
    for copy in [l_core, *l_chip, *l_layer]:
        copy.wait_send()
    for t in range(LAYERS):
        @pl.when(t > layer)
        def _(t=t):
            for q in range(CHIPS):
                code_copy(q, t).wait_send()

        @pl.when(t < layer)
        def _(t=t):
            for i in range(len(GROUPS)):
                grad_copy(i, t).wait_send()


def fused(residual, target, enc_weight, enc_bias, dec_weight, active):
    bf, f32 = jnp.bfloat16, jnp.float32
    vmem, dma = pltpu.VMEM, pltpu.SemaphoreType.DMA
    in_hbm = pl.BlockSpec(memory_space=pltpu.HBM)
    in_vmem = pl.BlockSpec(memory_space=pltpu.VMEM)
    loss, enc_grad, bias_grad, dec_grad = pl.pallas_call(
        fused_kernel,
        out_shape=[
            jax.ShapeDtypeStruct((1, 1), f32),
            jax.ShapeDtypeStruct(enc_weight.shape, bf),
            jax.ShapeDtypeStruct(enc_bias.shape, f32),
            jax.ShapeDtypeStruct(dec_weight.shape, bf),
        ],
        in_specs=[in_hbm] * 5 + [pl.BlockSpec(memory_space=pltpu.SMEM)],
        out_specs=[in_vmem] * 4,
        scratch_shapes=[
            vmem((TOKENS, D), bf),
            vmem((D, TOKENS), bf),
            vmem((D, BLOCK), bf),
            vmem((LAYERS, BLOCK, D), bf),
            vmem((TILE, D), bf),
            vmem((1, BLOCK), f32),
            vmem((TOKENS, BLOCK), f32),
            vmem((TOKENS, LAYERS * BLOCK), bf),
            vmem((2, CHUNKS, 2, 2, TILE, CW), bf),
            vmem((2, CHUNKS, 2, TILE, CW), bf),
            vmem((CHUNKS, CHIPS, TILE, CW), bf),
            vmem((CHUNKS, CHIPS, TILE, CW), bf),
            vmem((TOKENS, D), bf),
            vmem((TOKENS, LAYERS * BLOCK), f32),
            vmem((TOKENS, LAYERS * BLOCK), bf),
            vmem((LAYERS, TOKENS, BLOCK), bf),
            vmem((TOKENS, BLOCK), f32),
            vmem((2, 8, 128), f32),
            vmem((CHIPS, 8, 128), f32),
            vmem((LAYERS, 8, 128), f32),
            dma((5,)),
            dma((CHIPS,)),
            dma((CHIPS,)),
            dma((CHIPS,)),
            dma((CHIPS,)),
            dma((LAYERS, CHIPS)),
            dma((LAYERS, CHIPS)),
            dma((2, CHUNKS)),
            dma((2, CHUNKS)),
            dma((CHUNKS, CHIPS)),
            dma((CHUNKS, CHIPS)),
            dma((CHUNKS, CHIPS)),
            dma((CHUNKS, CHIPS)),
            dma((CHUNKS, CHIPS)),
            dma((CHUNKS, CHIPS)),
            dma((LAYERS, len(GROUPS))),
            dma((LAYERS, len(GROUPS))),
            dma((CHIPS + LAYERS - 1,)),
            dma((CHIPS + LAYERS - 1,)),
        ],
        compiler_params=pltpu.CompilerParams(
            collective_id=0, has_side_effects=True, vmem_limit_bytes=47 * 2**20
        ),
        cost_estimate=pl.CostEstimate(
            flops=14 * 2 * TOKENS * D * BLOCK, bytes_accessed=10 * 2**20, transcendentals=0
        ),
        name="transcoder_step",
    )(residual, target, enc_weight, enc_bias, dec_weight, jnp.swapaxes(active, 1, 2))
    return (
        loss[0, 0] * (0.5 / (LAYERS * TOKENS * D)),
        enc_grad * jnp.asarray(1.0 / TILE, bf),
        bias_grad * (1.0 / TILE),
        dec_grad * jnp.asarray(1.0 / TILE, bf),
    )


def shifted(value, axis, steps):
    count = lax.axis_size(axis)
    leading, last = (max(0, -steps), min(count, count - steps))
    return lax.ppermute(value, axis, [(source, source + steps) for source in range(leading, last)])


def slot_list(active, layer, my_block, slot_count):
    block_ids = lax.dynamic_index_in_dim(active, layer, 0, keepdims=False)
    hit = jnp.any(block_ids == my_block, axis=1).astype(jnp.int32)
    every = jnp.arange(NTILE, dtype=jnp.int32)
    place = jnp.cumsum(hit) - 1
    chosen = (hit[None, :] == 1) & (
        place[None, :] == jnp.arange(slot_count, dtype=jnp.int32)[:, None]
    )
    tile_ids = jnp.sum(jnp.where(chosen, every[None, :], 0), axis=1)
    filled = jnp.sum(chosen.astype(jnp.float32), axis=1)
    return (tile_ids, filled)


def shards(residual, target, enc_weight, enc_bias, dec_weight, active):
    layers = dec_weight.shape[0]
    feat_dev = enc_weight.shape[2]
    layer_index = lax.axis_index("layer")
    my_block = lax.axis_index("latent") * feat_dev // BLOCK
    slot_count = CAP
    slot_rows = slot_count * TILE
    full_inputs = lax.all_gather(residual[0], "latent", axis=0, tiled=True).reshape(NTILE, TILE, D)
    own_tiles, own_filled = slot_list(active, layer_index, my_block, slot_count)
    rows = jnp.take(full_inputs, own_tiles, axis=0).reshape(slot_rows, D)
    preact = jnp.dot(rows, enc_weight[0], preferred_element_type=jnp.float32) + enc_bias[0][None, :]
    live = jnp.repeat(own_filled, TILE)[:, None]
    sparse_codes = (jnp.maximum(preact, 0.0) * live).astype(jnp.bfloat16)
    dec_all = dec_weight[:, 0]

    def take_source(carry, portion, source):
        writes, kept = carry
        usable = (source >= 0) & (source <= layer_index)
        source_idx = jnp.clip(source, 0, layers - 1)
        portion = jnp.where(usable, portion, jnp.zeros_like(portion))
        tile_ids, _ = slot_list(active, source_idx, my_block, slot_count)
        weight = lax.dynamic_index_in_dim(dec_all, source_idx, 0, keepdims=False)
        product = jnp.dot(portion, weight, preferred_element_type=jnp.float32).reshape(
            slot_count, TILE, D
        )
        writes = writes.at[tile_ids].add(product)
        kept = jnp.where(usable, kept.at[source_idx].set(portion), kept)
        return (writes, kept)

    start_state = (
        jnp.zeros((NTILE, TILE, D), jnp.float32),
        jnp.zeros((layers, slot_rows, feat_dev), jnp.bfloat16),
    )
    state = take_source(start_state, sparse_codes, layer_index)
    moving = sparse_codes
    for hop in range(1, layers):
        moving = shifted(moving, "layer", 1)
        state = take_source(state, moving, layer_index - hop)
    writes, kept = state
    recon = lax.psum_scatter(
        writes.reshape(NTILE * TILE, D), "latent", scatter_dimension=0, tiled=True
    )
    errors = recon - target[0].astype(jnp.float32)
    total = lax.psum(jnp.sum(errors * errors), ("layer", "latent"))
    loss = 0.5 * total / (layers * NTILE * TILE * D)
    full_errors = lax.all_gather(errors.astype(jnp.bfloat16), "latent", axis=0, tiled=True).reshape(
        NTILE, TILE, D
    )
    dec_grads = []
    code_grads = []
    for source in range(layers):
        tile_ids, _ = slot_list(active, source, my_block, slot_count)
        error_part = jnp.take(full_errors, tile_ids, axis=0).reshape(slot_rows, D)
        grad = lax.dot_general(
            kept[source], error_part, (((0,), (0,)), ((), ())), preferred_element_type=jnp.float32
        )
        dec_grads.append((grad / TILE).astype(jnp.bfloat16))
        back = lax.dot_general(
            error_part,
            dec_all[source],
            (((1,), (1,)), ((), ())),
            preferred_element_type=jnp.float32,
        )
        code_grads.append(jnp.where(source <= layer_index, back, jnp.zeros_like(back)))
    dec_grad = jnp.stack(dec_grads)[:, None]
    code_grad = jnp.stack(code_grads)
    running = code_grad
    for hop in range(1, layers):
        running = code_grad + shifted(running, "layer", -1)
    mine = lax.dynamic_index_in_dim(running, layer_index, 0, keepdims=False)
    pre_grad = jnp.where(preact > 0, mine, jnp.zeros_like(mine)) * live
    bias_grad = (jnp.sum(pre_grad, axis=0) / TILE)[None]
    enc_term = lax.dot_general(
        rows,
        pre_grad.astype(jnp.bfloat16),
        (((0,), (0,)), ((), ())),
        preferred_element_type=jnp.float32,
    )
    enc_grad = (enc_term / TILE).astype(jnp.bfloat16)[None]
    return (loss, enc_grad, bias_grad, dec_grad)


def solution(mesh):
    in_specs = (
        P("layer", "latent", None),
        P("layer", "latent", None),
        P("layer", None, "latent"),
        P("layer", "latent"),
        P(None, "layer", "latent", None),
        P(),
    )
    out_specs = (
        P(),
        P("layer", None, "latent"),
        P("layer", "latent"),
        P(None, "layer", "latent", None),
    )
    one_tile_each = mesh.shape["latent"] == NTILE and mesh.shape["layer"] == LAYERS
    step = fused if one_tile_each else shards
    return jax.shard_map(step, mesh=mesh, in_specs=in_specs, out_specs=out_specs, check_vma=False)
```

```python
import functools

import jax
import jax.numpy as jnp
from jax import lax
from jax.experimental import pallas as pl
from jax.experimental.pallas import tpu as pltpu
from jax.sharding import PartitionSpec as P

D = 1792
BLOCK = 256
TILE = 64
NTILE = 8
CAP = 6
CHIPS = NTILE // 2
PAIR = 2 * TILE
TOKENS = NTILE * TILE
LAYERS = 4
CHUNKS = 2
CW = D // CHUNKS
MESH = pl.DeviceIdType.MESH
GROUPS = ((0, 2 * PAIR), (2 * PAIR, PAIR), (3 * PAIR, PAIR))


def fused_kernel(
    res, tgt, enc_w, bias, dec_w, active,
    loss, enc_g, bias_g, dec_g,
    x, xt, we, wd, goal, offset, masked, codes, part, part_in, shares, share_in, err,
    grad, grad_bf, grad_in, acc, dec_v, enc_v, sum_core, sum_chip, sum_layer,
    load_sem, store_sem, x_send, x_recv, xp_send, xp_recv, c_send, c_recv,
    p_send, p_recv, s_send, s_recv, e_send, e_recv, ep_send, ep_recv, g_send, g_recv,
    l_send, l_recv,
):
    layer = lax.axis_index("layer")
    latent = lax.axis_index("latent")
    z = latent // 2
    core = latent % 2
    middle = (z * (CHIPS - 1 - z)) // 2
    mates = (z, z + 1 - 2 * (z % 2), (z + 2) % CHIPS, CHIPS - 1 - z)
    partner = (layer, 2 * z + 1 - core)

    def chip(m):
        return (layer, 2 * mates[m] + core)

    def half(slot):
        return pl.ds(pl.multiple_of(slot * PAIR + core * TILE, TILE), TILE)

    def remote(src, dst, send, recv, device):
        return pltpu.make_async_remote_copy(
            src_ref=src, dst_ref=dst, send_sem=send, recv_sem=recv,
            device_id=device, device_id_type=MESH,
        )

    own_cols = pl.ds(pl.multiple_of(layer * BLOCK, BLOCK), BLOCK)
    loads = [
        pltpu.make_async_copy(res.at[0], x.at[half(0)], load_sem.at[0]),
        pltpu.make_async_copy(enc_w.at[0], we, load_sem.at[1]),
        pltpu.make_async_copy(bias, offset, load_sem.at[4]),
        pltpu.make_async_copy(dec_w.at[:, 0], wd, load_sem.at[2]),
        pltpu.make_async_copy(tgt.at[0], goal, load_sem.at[3]),
    ]
    for load in loads:
        load.start()

    barrier = pltpu.get_barrier_semaphore()
    pl.semaphore_signal(barrier, inc=1, device_id=partner, device_id_type=MESH)
    for m in range(1, CHIPS):
        pl.semaphore_signal(barrier, inc=1, device_id=chip(m), device_id_type=MESH)
    for d in range(1, LAYERS):
        pl.semaphore_signal(
            barrier, inc=1, device_id=(lax.rem(layer + d, LAYERS), latent), device_id_type=MESH
        )
    pl.semaphore_wait(barrier, 1 + CHIPS - 1 + LAYERS - 1)

    x_out = {
        m: remote(res.at[0], x.at[half(m)], x_send.at[m], x_recv.at[m], chip(m))
        for m in (1, 2, 3)
    }
    x_far = remote(x.at[half(2)], x.at[half(3)], x_send.at[0], x_recv.at[3], chip(1))
    xp_out = {0: remote(res.at[0], x.at[half(0)], xp_send.at[0], xp_recv.at[0], partner)}
    xp_out[0].start()
    for m in (1, 2):
        x_out[m].start()

    for s in range(1, LAYERS):
        @pl.when(s > layer)
        def _(s=s):
            codes[:, s * BLOCK:(s + 1) * BLOCK] = jnp.zeros((TOKENS, BLOCK), jnp.bfloat16)

    @pl.when(middle == 0)
    def _():
        for j in range(CHUNKS):
            share_in[j, 3] = jnp.zeros((TILE, CW), jnp.bfloat16)

    def code_copy(q, t):
        block = codes.at[pl.ds(q * PAIR, PAIR), own_cols]
        return remote(block, block, c_send.at[t, q], c_recv.at[layer, q], (t, latent))

    def code_wait(q):
        for s in range(LAYERS - 1):
            @pl.when(s < layer)
            def _(s=s):
                block = codes.at[pl.ds(q * PAIR, PAIR), pl.ds(s * BLOCK, BLOCK)]
                remote(
                    block, block, c_send.at[s, q], c_recv.at[s, q], (s, latent)
                ).wait_recv()

    def encode(q):
        rows = pl.ds(q * PAIR, PAIR)
        pre = jnp.dot(x[rows, :], we[...], preferred_element_type=jnp.float32) + offset[...]
        for c in range(2):
            listed = [active[layer, a, 2 * mates[q] + c] for a in range(active.shape[1])]
            hit = functools.reduce(jnp.logical_or, [b == latent for b in listed])
            live = jnp.where(hit, 1.0, 0.0).astype(jnp.float32)
            kept = pre[c * TILE:(c + 1) * TILE] * live
            spot = pl.ds(q * PAIR + c * TILE, TILE)
            masked[spot, :] = kept
            codes[spot, own_cols] = jnp.maximum(kept, 0.0).astype(jnp.bfloat16)
        for t in range(1, LAYERS):
            @pl.when(t > layer)
            def _(t=t):
                code_copy(q, t).start()

    def take_x(m):
        x_out[m].wait_recv()
        xp_out[m] = remote(x.at[half(m)], x.at[half(m)], xp_send.at[m], xp_recv.at[m], partner)
        xp_out[m].start()

    p_out, s_out = {}, {}

    def decode(first, count):
        for j in range(CHUNKS):
            full = jnp.dot(
                codes[first * PAIR:(first + count) * PAIR, :],
                wd[:, :, j * CW:(j + 1) * CW].reshape(LAYERS * BLOCK, CW),
                preferred_element_type=jnp.float32,
            ).astype(jnp.bfloat16)
            for q in range(count):
                for c in range(2):
                    at = q * PAIR + c * TILE
                    part[first + q, c, :, j * CW:(j + 1) * CW] = full[at:at + TILE]
        for q in range(first, first + count):
            p_out[q] = remote(
                part.at[q, 1 - core], part_in.at[q], p_send.at[q], p_recv.at[q], partner
            )
            p_out[q].start()

    def chip_sum(j, m):
        cols = slice(j * CW, (j + 1) * CW)
        own = part[m, core, :, cols].astype(jnp.float32)
        return own + part_in[m, :, cols].astype(jnp.float32)

    def send_share(j, m, slot, device):
        s_out[j, m] = remote(
            shares.at[j, m], share_in.at[j, slot], s_send.at[j, m], s_recv.at[j, slot], device
        )
        s_out[j, m].start()

    def share_wait(j, slot):
        remote(
            shares.at[j, slot], share_in.at[j, slot], s_send.at[j, slot], s_recv.at[j, slot],
            partner,
        ).wait_recv()

    loads[0].wait()
    loads[1].wait()
    loads[2].wait()
    xp_out[0].wait_recv()
    encode(0)
    take_x(1)
    take_x(2)

    @pl.when(middle == 1)
    def _():
        x_far.start()
        x_out[3].start()

    xp_out[1].wait_recv()
    encode(1)
    xp_out[2].wait_recv()
    encode(2)
    loads[3].wait()
    code_wait(0)
    code_wait(1)
    decode(0, 2)
    take_x(3)
    p_out[0].wait_recv()
    p_out[1].wait_recv()
    for j in range(CHUNKS):
        shares[j, 1] = chip_sum(j, 1).astype(jnp.bfloat16)
        send_share(j, 1, 1, chip(1))
    code_wait(2)
    decode(2, 1)
    xp_out[3].wait_recv()
    encode(3)
    p_out[2].wait_recv()
    for j in range(CHUNKS):
        shares[j, 2] = chip_sum(j, 2).astype(jnp.bfloat16)
        s_out[j, 2] = remote(
            shares.at[j, 2], share_in.at[j, 2], s_send.at[j, 2], s_recv.at[j, 2], chip(2)
        )

        @pl.when(middle == 0)
        def _(j=j):
            s_out[j, 2].start()

    code_wait(3)
    decode(3, 1)
    far = (layer, 2 * (middle * mates[3] + (1 - middle) * mates[1]) + core)
    p_out[3].wait_recv()
    for j in range(CHUNKS):
        shares[j, 3] = chip_sum(j, 3).astype(jnp.bfloat16)
        send_share(j, 3, 3 * middle, far)

    @pl.when(middle == 1)
    def _():
        for j in range(CHUNKS):
            share_wait(j, 0)
            shares[j, 2] = (
                chip_sum(j, 2) + share_in[j, 0].astype(jnp.float32)
            ).astype(jnp.bfloat16)
            s_out[j, 2].start()

    xt[...] = x[...].T

    loads[4].wait()
    e_out, ep_out, e_far = {}, {}, {}
    squares = jnp.zeros((8, 128), jnp.float32)
    for j in range(CHUNKS):
        cols = pl.ds(j * CW, CW)
        share_wait(j, 1)
        share_wait(j, 2)

        @pl.when(middle == 1)
        def _(j=j):
            share_wait(j, 3)

        total = chip_sum(j, 0)
        for m in (1, 2, 3):
            total = total + share_in[j, m].astype(jnp.float32)
        error = total - goal[:, j * CW:(j + 1) * CW].astype(jnp.float32)
        err[half(0), cols] = error.astype(jnp.bfloat16)
        block = err.at[half(0), cols]
        for m in (1, 2, 3):
            e_out[j, m] = remote(
                block, err.at[half(m), cols], e_send.at[j, m], e_recv.at[j, m], chip(m)
            )
        e_far[j] = remote(
            err.at[half(2), cols], err.at[half(3), cols], e_send.at[j, 0], e_recv.at[j, 3], chip(1)
        )
        for m in (2, 1):
            e_out[j, m].start()
        ep_out[j, 0] = remote(block, block, ep_send.at[j, 0], ep_recv.at[j, 0], partner)
        ep_out[j, 0].start()
        square = jnp.sum((error * error).reshape(TILE // 8, 8, CW), axis=0)
        for b in range(CW // 128):
            squares = squares + square[:, b * 128:(b + 1) * 128]

    sum_core[core] = squares
    l_core = remote(sum_core.at[core], sum_core.at[core], l_send.at[0], l_recv.at[0], partner)
    l_core.start()

    def take_e(j, m):
        e_out[j, m].wait_recv()
        block = err.at[half(m), pl.ds(j * CW, CW)]
        ep_out[j, m] = remote(block, block, ep_send.at[j, m], ep_recv.at[j, m], partner)
        ep_out[j, m].start()

    def grad_copy(i, s):
        rows = pl.ds(*GROUPS[i])
        return remote(
            grad_bf.at[rows, pl.ds(s * BLOCK, BLOCK)], grad_in.at[layer, rows],
            g_send.at[s, i], g_recv.at[layer, i], (s, latent),
        )

    def grad_wait(i, t):
        rows = pl.ds(*GROUPS[i])
        remote(
            grad_bf.at[rows, pl.ds(0, BLOCK)], grad_in.at[t, rows],
            g_send.at[t, i], g_recv.at[t, i], (t, latent),
        ).wait_recv()

    def code_grad(i):
        rows = pl.ds(*GROUPS[i])
        back = lax.dot_general(
            err[rows, :], wd[...].reshape(LAYERS * BLOCK, D),
            (((1,), (1,)), ((), ())), preferred_element_type=jnp.float32,
        )
        grad[rows, :] = back
        grad_bf[rows, :] = back.astype(jnp.bfloat16)
        for s in range(LAYERS - 1):
            @pl.when(s < layer)
            def _(s=s):
                grad_copy(i, s).start()

    for j in range(CHUNKS):
        take_e(j, 2)

        @pl.when(middle == 1)
        def _(j=j):
            e_far[j].start()
            e_out[j, 3].start()

        take_e(j, 1)
    l_core.wait_recv()
    sum_chip[z] = sum_core[0] + sum_core[1]
    l_chip = [
        remote(sum_chip.at[z], sum_chip.at[z], l_send.at[m], l_recv.at[m], chip(m))
        for m in range(1, CHIPS)
    ]
    for copy in l_chip:
        copy.start()
    for m in (0, 1):
        for j in range(CHUNKS):
            ep_out[j, m].wait_recv()
    code_grad(0)
    for j in range(CHUNKS):
        ep_out[j, 2].wait_recv()
    code_grad(1)
    for copy in l_chip:
        copy.wait_recv()
    sum_layer[layer] = functools.reduce(jnp.add, [sum_chip[i] for i in range(CHIPS)])
    l_layer = [
        remote(
            sum_layer.at[layer], sum_layer.at[layer],
            l_send.at[CHIPS - 1 + d], l_recv.at[CHIPS - 1 + d],
            (lax.rem(layer + d, LAYERS), latent),
        )
        for d in range(1, LAYERS)
    ]
    for copy in l_layer:
        copy.start()
    for j in range(CHUNKS):
        take_e(j, 3)
    for j in range(CHUNKS):
        ep_out[j, 3].wait_recv()
    code_grad(2)

    stores = []
    for s in range(LAYERS):
        dec_v[s] = lax.dot_general(
            codes[:, s * BLOCK:(s + 1) * BLOCK], err[...],
            (((0,), (0,)), ((), ())), preferred_element_type=jnp.float32,
        ).astype(jnp.bfloat16)
        stores.append(pltpu.make_async_copy(dec_v.at[s], dec_g.at[s, 0], store_sem.at[s]))
        stores[s].start()

    acc[...] = grad[:, own_cols]
    for t in range(1, LAYERS):
        @pl.when(t > layer)
        def _(t=t):
            for i in range(len(GROUPS)):
                grad_wait(i, t)
            acc[...] += grad_in[t].astype(jnp.float32)
    pre_grad = jnp.where(masked[...] > 0, acc[...], 0.0)
    bias_g[...] = jnp.sum(pre_grad, axis=0, keepdims=True)
    enc_v[...] = jnp.dot(
        xt[...], pre_grad.astype(jnp.bfloat16), preferred_element_type=jnp.float32
    ).astype(jnp.bfloat16)
    stores.append(pltpu.make_async_copy(enc_v, enc_g.at[0], store_sem.at[LAYERS]))
    stores[LAYERS].start()

    for copy in l_layer:
        copy.wait_recv()
    every = functools.reduce(jnp.add, [sum_layer[i] for i in range(LAYERS)])
    loss[...] = jnp.sum(every, keepdims=True)

    for m in (1, 2):
        x_out[m].wait_send()
        for j in range(CHUNKS):
            e_out[j, m].wait_send()

    @pl.when(middle == 1)
    def _():
        for copy in [x_far, x_out[3], *e_far.values(), *[e_out[j, 3] for j in range(CHUNKS)]]:
            copy.wait_send()

    for copies in (xp_out, p_out, s_out, ep_out):
        for copy in copies.values():
            copy.wait_send()
    for copy in [l_core, *l_chip, *l_layer]:
        copy.wait_send()
    for t in range(LAYERS):
        @pl.when(t > layer)
        def _(t=t):
            for q in range(CHIPS):
                code_copy(q, t).wait_send()

        @pl.when(t < layer)
        def _(t=t):
            for i in range(len(GROUPS)):
                grad_copy(i, t).wait_send()
    for store in stores:
        store.wait()


def fused(residual, target, enc_weight, enc_bias, dec_weight, active):
    bf, f32 = jnp.bfloat16, jnp.float32
    vmem, dma = pltpu.VMEM, pltpu.SemaphoreType.DMA
    in_hbm = pl.BlockSpec(memory_space=pltpu.HBM)
    in_vmem = pl.BlockSpec(memory_space=pltpu.VMEM)
    loss, enc_grad, bias_grad, dec_grad = pl.pallas_call(
        fused_kernel,
        out_shape=[
            jax.ShapeDtypeStruct((1, 1), f32),
            jax.ShapeDtypeStruct(enc_weight.shape, bf),
            jax.ShapeDtypeStruct(enc_bias.shape, f32),
            jax.ShapeDtypeStruct(dec_weight.shape, bf),
        ],
        in_specs=[in_hbm] * 5 + [pl.BlockSpec(memory_space=pltpu.SMEM)],
        out_specs=[in_vmem, in_hbm, in_vmem, in_hbm],
        scratch_shapes=[
            vmem((TOKENS, D), bf),
            vmem((D, TOKENS), bf),
            vmem((D, BLOCK), bf),
            vmem((LAYERS, BLOCK, D), bf),
            vmem((TILE, D), bf),
            vmem((1, BLOCK), f32),
            vmem((TOKENS, BLOCK), f32),
            vmem((TOKENS, LAYERS * BLOCK), bf),
            vmem((CHIPS, 2, TILE, D), bf),
            vmem((CHIPS, TILE, D), bf),
            vmem((CHUNKS, CHIPS, TILE, CW), bf),
            vmem((CHUNKS, CHIPS, TILE, CW), bf),
            vmem((TOKENS, D), bf),
            vmem((TOKENS, LAYERS * BLOCK), f32),
            vmem((TOKENS, LAYERS * BLOCK), bf),
            vmem((LAYERS, TOKENS, BLOCK), bf),
            vmem((TOKENS, BLOCK), f32),
            vmem((LAYERS, BLOCK, D), bf),
            vmem((D, BLOCK), bf),
            vmem((2, 8, 128), f32),
            vmem((CHIPS, 8, 128), f32),
            vmem((LAYERS, 8, 128), f32),
            dma((5,)),
            dma((LAYERS + 1,)),
            dma((CHIPS,)),
            dma((CHIPS,)),
            dma((CHIPS,)),
            dma((CHIPS,)),
            dma((LAYERS, CHIPS)),
            dma((LAYERS, CHIPS)),
            dma((CHIPS,)),
            dma((CHIPS,)),
            dma((CHUNKS, CHIPS)),
            dma((CHUNKS, CHIPS)),
            dma((CHUNKS, CHIPS)),
            dma((CHUNKS, CHIPS)),
            dma((CHUNKS, CHIPS)),
            dma((CHUNKS, CHIPS)),
            dma((LAYERS, len(GROUPS))),
            dma((LAYERS, len(GROUPS))),
            dma((CHIPS + LAYERS - 1,)),
            dma((CHIPS + LAYERS - 1,)),
        ],
        compiler_params=pltpu.CompilerParams(
            collective_id=0, has_side_effects=True, vmem_limit_bytes=56 * 2**20
        ),
        cost_estimate=pl.CostEstimate(
            flops=14 * 2 * TOKENS * D * BLOCK, bytes_accessed=10 * 2**20, transcendentals=0
        ),
        name="transcoder_step",
    )(residual, target, enc_weight, enc_bias, dec_weight, jnp.swapaxes(active, 1, 2))
    return (
        loss[0, 0] * (0.5 / (LAYERS * TOKENS * D)),
        enc_grad * jnp.asarray(1.0 / TILE, bf),
        bias_grad * (1.0 / TILE),
        dec_grad * jnp.asarray(1.0 / TILE, bf),
    )


def shifted(value, axis, steps):
    count = lax.axis_size(axis)
    leading, last = (max(0, -steps), min(count, count - steps))
    return lax.ppermute(value, axis, [(source, source + steps) for source in range(leading, last)])


def slot_list(active, layer, my_block, slot_count):
    block_ids = lax.dynamic_index_in_dim(active, layer, 0, keepdims=False)
    hit = jnp.any(block_ids == my_block, axis=1).astype(jnp.int32)
    every = jnp.arange(NTILE, dtype=jnp.int32)
    place = jnp.cumsum(hit) - 1
    chosen = (hit[None, :] == 1) & (
        place[None, :] == jnp.arange(slot_count, dtype=jnp.int32)[:, None]
    )
    tile_ids = jnp.sum(jnp.where(chosen, every[None, :], 0), axis=1)
    filled = jnp.sum(chosen.astype(jnp.float32), axis=1)
    return (tile_ids, filled)


def shards(residual, target, enc_weight, enc_bias, dec_weight, active):
    layers = dec_weight.shape[0]
    feat_dev = enc_weight.shape[2]
    layer_index = lax.axis_index("layer")
    my_block = lax.axis_index("latent") * feat_dev // BLOCK
    slot_count = CAP
    slot_rows = slot_count * TILE
    full_inputs = lax.all_gather(residual[0], "latent", axis=0, tiled=True).reshape(NTILE, TILE, D)
    own_tiles, own_filled = slot_list(active, layer_index, my_block, slot_count)
    rows = jnp.take(full_inputs, own_tiles, axis=0).reshape(slot_rows, D)
    preact = jnp.dot(rows, enc_weight[0], preferred_element_type=jnp.float32) + enc_bias[0][None, :]
    live = jnp.repeat(own_filled, TILE)[:, None]
    sparse_codes = (jnp.maximum(preact, 0.0) * live).astype(jnp.bfloat16)
    dec_all = dec_weight[:, 0]

    def take_source(carry, portion, source):
        writes, kept = carry
        usable = (source >= 0) & (source <= layer_index)
        source_idx = jnp.clip(source, 0, layers - 1)
        portion = jnp.where(usable, portion, jnp.zeros_like(portion))
        tile_ids, _ = slot_list(active, source_idx, my_block, slot_count)
        weight = lax.dynamic_index_in_dim(dec_all, source_idx, 0, keepdims=False)
        product = jnp.dot(portion, weight, preferred_element_type=jnp.float32).reshape(
            slot_count, TILE, D
        )
        writes = writes.at[tile_ids].add(product)
        kept = jnp.where(usable, kept.at[source_idx].set(portion), kept)
        return (writes, kept)

    start_state = (
        jnp.zeros((NTILE, TILE, D), jnp.float32),
        jnp.zeros((layers, slot_rows, feat_dev), jnp.bfloat16),
    )
    state = take_source(start_state, sparse_codes, layer_index)
    moving = sparse_codes
    for hop in range(1, layers):
        moving = shifted(moving, "layer", 1)
        state = take_source(state, moving, layer_index - hop)
    writes, kept = state
    recon = lax.psum_scatter(
        writes.reshape(NTILE * TILE, D), "latent", scatter_dimension=0, tiled=True
    )
    errors = recon - target[0].astype(jnp.float32)
    total = lax.psum(jnp.sum(errors * errors), ("layer", "latent"))
    loss = 0.5 * total / (layers * NTILE * TILE * D)
    full_errors = lax.all_gather(errors.astype(jnp.bfloat16), "latent", axis=0, tiled=True).reshape(
        NTILE, TILE, D
    )
    dec_grads = []
    code_grads = []
    for source in range(layers):
        tile_ids, _ = slot_list(active, source, my_block, slot_count)
        error_part = jnp.take(full_errors, tile_ids, axis=0).reshape(slot_rows, D)
        grad = lax.dot_general(
            kept[source], error_part, (((0,), (0,)), ((), ())), preferred_element_type=jnp.float32
        )
        dec_grads.append((grad / TILE).astype(jnp.bfloat16))
        back = lax.dot_general(
            error_part,
            dec_all[source],
            (((1,), (1,)), ((), ())),
            preferred_element_type=jnp.float32,
        )
        code_grads.append(jnp.where(source <= layer_index, back, jnp.zeros_like(back)))
    dec_grad = jnp.stack(dec_grads)[:, None]
    code_grad = jnp.stack(code_grads)
    running = code_grad
    for hop in range(1, layers):
        running = code_grad + shifted(running, "layer", -1)
    mine = lax.dynamic_index_in_dim(running, layer_index, 0, keepdims=False)
    pre_grad = jnp.where(preact > 0, mine, jnp.zeros_like(mine)) * live
    bias_grad = (jnp.sum(pre_grad, axis=0) / TILE)[None]
    enc_term = lax.dot_general(
        rows,
        pre_grad.astype(jnp.bfloat16),
        (((0,), (0,)), ((), ())),
        preferred_element_type=jnp.float32,
    )
    enc_grad = (enc_term / TILE).astype(jnp.bfloat16)[None]
    return (loss, enc_grad, bias_grad, dec_grad)


def solution(mesh):
    in_specs = (
        P("layer", "latent", None),
        P("layer", "latent", None),
        P("layer", None, "latent"),
        P("layer", "latent"),
        P(None, "layer", "latent", None),
        P(),
    )
    out_specs = (
        P(),
        P("layer", None, "latent"),
        P("layer", "latent"),
        P(None, "layer", "latent", None),
    )
    one_tile_each = mesh.shape["latent"] == NTILE and mesh.shape["layer"] == LAYERS
    step = fused if one_tile_each else shards
    return jax.shard_map(step, mesh=mesh, in_specs=in_specs, out_specs=out_specs, check_vma=False)
```

```python
import functools

import jax
import jax.numpy as jnp
from jax import lax
from jax.experimental import pallas as pl
from jax.experimental.pallas import tpu as pltpu
from jax.sharding import PartitionSpec as P

D = 1792
BLOCK = 256
TILE = 64
NTILE = 8
CAP = 6
CHIPS = NTILE // 2
PAIR = 2 * TILE
TOKENS = NTILE * TILE
LAYERS = 4
CHUNKS = 2
CW = D // CHUNKS
MESH = pl.DeviceIdType.MESH
GROUPS = ((0, 2 * PAIR), (2 * PAIR, PAIR), (3 * PAIR, PAIR))


def fused_kernel(
    res, tgt, enc_w, bias, dec_w, active,
    loss, enc_g, bias_g, dec_g,
    x, xt, we, wd, goal, offset, masked, codes, part, part_in, shares, share_in, err,
    grad, grad_bf, grad_in, acc, dec_acc, sum_core, sum_chip, sum_layer,
    load_sem, x_send, x_recv, xp_send, xp_recv, c_send, c_recv,
    p_send, p_recv, s_send, s_recv, e_send, e_recv, ep_send, ep_recv, g_send, g_recv,
    l_send, l_recv,
):
    layer = lax.axis_index("layer")
    latent = lax.axis_index("latent")
    z = latent // 2
    core = latent % 2
    middle = (z * (CHIPS - 1 - z)) // 2
    mates = (z, z + 1 - 2 * (z % 2), (z + 2) % CHIPS, CHIPS - 1 - z)
    partner = (layer, 2 * z + 1 - core)

    def chip(m):
        return (layer, 2 * mates[m] + core)

    def half(slot):
        return pl.ds(pl.multiple_of(slot * PAIR + core * TILE, TILE), TILE)

    def remote(src, dst, send, recv, device):
        return pltpu.make_async_remote_copy(
            src_ref=src, dst_ref=dst, send_sem=send, recv_sem=recv,
            device_id=device, device_id_type=MESH,
        )

    own_cols = pl.ds(pl.multiple_of(layer * BLOCK, BLOCK), BLOCK)
    loads = [
        pltpu.make_async_copy(res.at[0], x.at[half(0)], load_sem.at[0]),
        pltpu.make_async_copy(enc_w.at[0], we, load_sem.at[1]),
        pltpu.make_async_copy(bias, offset, load_sem.at[4]),
        pltpu.make_async_copy(dec_w.at[:, 0], wd, load_sem.at[2]),
        pltpu.make_async_copy(tgt.at[0], goal, load_sem.at[3]),
    ]
    for load in loads:
        load.start()

    barrier = pltpu.get_barrier_semaphore()
    pl.semaphore_signal(barrier, inc=1, device_id=partner, device_id_type=MESH)
    for m in range(1, CHIPS):
        pl.semaphore_signal(barrier, inc=1, device_id=chip(m), device_id_type=MESH)
    for d in range(1, LAYERS):
        pl.semaphore_signal(
            barrier, inc=1, device_id=(lax.rem(layer + d, LAYERS), latent), device_id_type=MESH
        )
    pl.semaphore_wait(barrier, 1 + CHIPS - 1 + LAYERS - 1)

    x_out = {
        m: remote(res.at[0], x.at[half(m)], x_send.at[m], x_recv.at[m], chip(m))
        for m in (1, 2, 3)
    }
    x_far = remote(x.at[half(2)], x.at[half(3)], x_send.at[0], x_recv.at[3], chip(1))
    xp_out = {0: remote(res.at[0], x.at[half(0)], xp_send.at[0], xp_recv.at[0], partner)}
    xp_out[0].start()
    for m in (1, 2):
        x_out[m].start()

    for s in range(1, LAYERS):
        @pl.when(s > layer)
        def _(s=s):
            codes[:, s * BLOCK:(s + 1) * BLOCK] = jnp.zeros((TOKENS, BLOCK), jnp.bfloat16)

    @pl.when(middle == 0)
    def _():
        for j in range(CHUNKS):
            share_in[j, 3] = jnp.zeros((TILE, CW), jnp.bfloat16)

    def code_copy(q, t):
        block = codes.at[pl.ds(q * PAIR, PAIR), own_cols]
        return remote(block, block, c_send.at[t, q], c_recv.at[layer, q], (t, latent))

    def code_wait(q):
        for s in range(LAYERS - 1):
            @pl.when(s < layer)
            def _(s=s):
                block = codes.at[pl.ds(q * PAIR, PAIR), pl.ds(s * BLOCK, BLOCK)]
                remote(
                    block, block, c_send.at[s, q], c_recv.at[s, q], (s, latent)
                ).wait_recv()

    def encode(q):
        rows = pl.ds(q * PAIR, PAIR)
        pre = jnp.dot(x[rows, :], we[...], preferred_element_type=jnp.float32) + offset[...]
        for c in range(2):
            listed = [active[layer, a, 2 * mates[q] + c] for a in range(active.shape[1])]
            hit = functools.reduce(jnp.logical_or, [b == latent for b in listed])
            live = jnp.where(hit, 1.0, 0.0).astype(jnp.float32)
            kept = pre[c * TILE:(c + 1) * TILE] * live
            spot = pl.ds(q * PAIR + c * TILE, TILE)
            masked[spot, :] = kept
            codes[spot, own_cols] = jnp.maximum(kept, 0.0).astype(jnp.bfloat16)
        for t in range(1, LAYERS):
            @pl.when(t > layer)
            def _(t=t):
                code_copy(q, t).start()

    def take_x(m):
        x_out[m].wait_recv()
        xp_out[m] = remote(x.at[half(m)], x.at[half(m)], xp_send.at[m], xp_recv.at[m], partner)
        xp_out[m].start()

    p_out, s_out = {}, {}

    def decode(first, count):
        for j in range(CHUNKS):
            full = jnp.dot(
                codes[first * PAIR:(first + count) * PAIR, :],
                wd[:, :, j * CW:(j + 1) * CW].reshape(LAYERS * BLOCK, CW),
                preferred_element_type=jnp.float32,
            ).astype(jnp.bfloat16)
            for q in range(count):
                for c in range(2):
                    at = q * PAIR + c * TILE
                    part[first + q, c, :, j * CW:(j + 1) * CW] = full[at:at + TILE]
        for q in range(first, first + count):
            p_out[q] = remote(
                part.at[q, 1 - core], part_in.at[q], p_send.at[q], p_recv.at[q], partner
            )
            p_out[q].start()

    def chip_sum(j, m):
        cols = slice(j * CW, (j + 1) * CW)
        own = part[m, core, :, cols].astype(jnp.float32)
        return own + part_in[m, :, cols].astype(jnp.float32)

    def send_share(j, m, slot, device):
        s_out[j, m] = remote(
            shares.at[j, m], share_in.at[j, slot], s_send.at[j, m], s_recv.at[j, slot], device
        )
        s_out[j, m].start()

    def share_wait(j, slot):
        remote(
            shares.at[j, slot], share_in.at[j, slot], s_send.at[j, slot], s_recv.at[j, slot],
            partner,
        ).wait_recv()

    loads[0].wait()
    loads[1].wait()
    loads[2].wait()
    xp_out[0].wait_recv()
    encode(0)
    take_x(1)
    take_x(2)

    @pl.when(middle == 1)
    def _():
        x_far.start()
        x_out[3].start()

    xp_out[1].wait_recv()
    encode(1)
    xp_out[2].wait_recv()
    encode(2)
    loads[3].wait()
    code_wait(0)
    code_wait(1)
    decode(0, 2)
    take_x(3)
    p_out[0].wait_recv()
    p_out[1].wait_recv()
    for j in range(CHUNKS):
        shares[j, 1] = chip_sum(j, 1).astype(jnp.bfloat16)
        send_share(j, 1, 1, chip(1))
    code_wait(2)
    decode(2, 1)
    xp_out[3].wait_recv()
    encode(3)
    p_out[2].wait_recv()
    for j in range(CHUNKS):
        shares[j, 2] = chip_sum(j, 2).astype(jnp.bfloat16)
        s_out[j, 2] = remote(
            shares.at[j, 2], share_in.at[j, 2], s_send.at[j, 2], s_recv.at[j, 2], chip(2)
        )

        @pl.when(middle == 0)
        def _(j=j):
            s_out[j, 2].start()

    code_wait(3)
    decode(3, 1)
    far = (layer, 2 * (middle * mates[3] + (1 - middle) * mates[1]) + core)
    p_out[3].wait_recv()
    for j in range(CHUNKS):
        shares[j, 3] = chip_sum(j, 3).astype(jnp.bfloat16)
        send_share(j, 3, 3 * middle, far)

    @pl.when(middle == 1)
    def _():
        for j in range(CHUNKS):
            share_wait(j, 0)
            shares[j, 2] = (
                chip_sum(j, 2) + share_in[j, 0].astype(jnp.float32)
            ).astype(jnp.bfloat16)
            s_out[j, 2].start()

    xt[...] = x[...].T

    loads[4].wait()
    e_out, ep_out, e_far = {}, {}, {}
    squares = jnp.zeros((8, 128), jnp.float32)
    for j in range(CHUNKS):
        cols = pl.ds(j * CW, CW)
        share_wait(j, 1)
        share_wait(j, 2)

        @pl.when(middle == 1)
        def _(j=j):
            share_wait(j, 3)

        total = chip_sum(j, 0)
        for m in (1, 2, 3):
            total = total + share_in[j, m].astype(jnp.float32)
        error = total - goal[:, j * CW:(j + 1) * CW].astype(jnp.float32)
        err[half(0), cols] = error.astype(jnp.bfloat16)
        block = err.at[half(0), cols]
        for m in (1, 2, 3):
            e_out[j, m] = remote(
                block, err.at[half(m), cols], e_send.at[j, m], e_recv.at[j, m], chip(m)
            )
        e_far[j] = remote(
            err.at[half(2), cols], err.at[half(3), cols], e_send.at[j, 0], e_recv.at[j, 3], chip(1)
        )
        for m in (2, 1):
            e_out[j, m].start()
        ep_out[j, 0] = remote(block, block, ep_send.at[j, 0], ep_recv.at[j, 0], partner)
        ep_out[j, 0].start()
        square = jnp.sum((error * error).reshape(TILE // 8, 8, CW), axis=0)
        for b in range(CW // 128):
            squares = squares + square[:, b * 128:(b + 1) * 128]

    sum_core[core] = squares
    l_core = remote(sum_core.at[core], sum_core.at[core], l_send.at[0], l_recv.at[0], partner)
    l_core.start()

    def take_e(j, m):
        e_out[j, m].wait_recv()
        block = err.at[half(m), pl.ds(j * CW, CW)]
        ep_out[j, m] = remote(block, block, ep_send.at[j, m], ep_recv.at[j, m], partner)
        ep_out[j, m].start()

    def grad_copy(i, s):
        rows = pl.ds(*GROUPS[i])
        return remote(
            grad_bf.at[rows, pl.ds(s * BLOCK, BLOCK)], grad_in.at[layer, rows],
            g_send.at[s, i], g_recv.at[layer, i], (s, latent),
        )

    def grad_wait(i, t):
        rows = pl.ds(*GROUPS[i])
        remote(
            grad_bf.at[rows, pl.ds(0, BLOCK)], grad_in.at[t, rows],
            g_send.at[t, i], g_recv.at[t, i], (t, latent),
        ).wait_recv()

    def code_grad(i):
        rows = pl.ds(*GROUPS[i])
        back = lax.dot_general(
            err[rows, :], wd[...].reshape(LAYERS * BLOCK, D),
            (((1,), (1,)), ((), ())), preferred_element_type=jnp.float32,
        )
        grad[rows, :] = back
        grad_bf[rows, :] = back.astype(jnp.bfloat16)
        for s in range(LAYERS - 1):
            @pl.when(s < layer)
            def _(s=s):
                grad_copy(i, s).start()

    def dec_term(s, first, count):
        return lax.dot_general(
            codes[first:first + count, s * BLOCK:(s + 1) * BLOCK], err[first:first + count, :],
            (((0,), (0,)), ((), ())), preferred_element_type=jnp.float32,
        )

    for j in range(CHUNKS):
        take_e(j, 2)

        @pl.when(middle == 1)
        def _(j=j):
            e_far[j].start()
            e_out[j, 3].start()

        take_e(j, 1)
    l_core.wait_recv()
    sum_chip[z] = sum_core[0] + sum_core[1]
    l_chip = [
        remote(sum_chip.at[z], sum_chip.at[z], l_send.at[m], l_recv.at[m], chip(m))
        for m in range(1, CHIPS)
    ]
    for copy in l_chip:
        copy.start()
    for m in (0, 1):
        for j in range(CHUNKS):
            ep_out[j, m].wait_recv()
    code_grad(0)
    for j in range(CHUNKS):
        ep_out[j, 2].wait_recv()
    code_grad(1)
    for copy in l_chip:
        copy.wait_recv()
    sum_layer[layer] = functools.reduce(jnp.add, [sum_chip[i] for i in range(CHIPS)])
    l_layer = [
        remote(
            sum_layer.at[layer], sum_layer.at[layer],
            l_send.at[CHIPS - 1 + d], l_recv.at[CHIPS - 1 + d],
            (lax.rem(layer + d, LAYERS), latent),
        )
        for d in range(1, LAYERS)
    ]
    for copy in l_layer:
        copy.start()
    dec_acc[0] = dec_term(0, 0, 3 * PAIR)
    dec_acc[1] = dec_term(1, 0, 3 * PAIR)
    for j in range(CHUNKS):
        take_e(j, 3)
    dec_acc[2] = dec_term(2, 0, 3 * PAIR)
    for j in range(CHUNKS):
        ep_out[j, 3].wait_recv()
    code_grad(2)

    for s in range(LAYERS):
        if s < 3:
            total = dec_acc[s] + dec_term(s, 3 * PAIR, PAIR)
        else:
            total = dec_term(s, 0, TOKENS)
        dec_g[s, 0] = total.astype(jnp.bfloat16)

    acc[...] = grad[:, own_cols]
    for t in range(1, LAYERS):
        @pl.when(t > layer)
        def _(t=t):
            for i in range(len(GROUPS)):
                grad_wait(i, t)
            acc[...] += grad_in[t].astype(jnp.float32)
    pre_grad = jnp.where(masked[...] > 0, acc[...], 0.0)
    bias_g[...] = jnp.sum(pre_grad, axis=0, keepdims=True)
    enc_g[0] = jnp.dot(
        xt[...], pre_grad.astype(jnp.bfloat16), preferred_element_type=jnp.float32
    ).astype(jnp.bfloat16)

    for copy in l_layer:
        copy.wait_recv()
    every = functools.reduce(jnp.add, [sum_layer[i] for i in range(LAYERS)])
    loss[...] = jnp.sum(every, keepdims=True)

    for m in (1, 2):
        x_out[m].wait_send()
        for j in range(CHUNKS):
            e_out[j, m].wait_send()

    @pl.when(middle == 1)
    def _():
        for copy in [x_far, x_out[3], *e_far.values(), *[e_out[j, 3] for j in range(CHUNKS)]]:
            copy.wait_send()

    for copies in (xp_out, p_out, s_out, ep_out):
        for copy in copies.values():
            copy.wait_send()
    for copy in [l_core, *l_chip, *l_layer]:
        copy.wait_send()
    for t in range(LAYERS):
        @pl.when(t > layer)
        def _(t=t):
            for q in range(CHIPS):
                code_copy(q, t).wait_send()

        @pl.when(t < layer)
        def _(t=t):
            for i in range(len(GROUPS)):
                grad_copy(i, t).wait_send()


def fused(residual, target, enc_weight, enc_bias, dec_weight, active):
    bf, f32 = jnp.bfloat16, jnp.float32
    vmem, dma = pltpu.VMEM, pltpu.SemaphoreType.DMA
    in_hbm = pl.BlockSpec(memory_space=pltpu.HBM)
    in_vmem = pl.BlockSpec(memory_space=pltpu.VMEM)
    loss, enc_grad, bias_grad, dec_grad = pl.pallas_call(
        fused_kernel,
        out_shape=[
            jax.ShapeDtypeStruct((1, 1), f32),
            jax.ShapeDtypeStruct(enc_weight.shape, bf),
            jax.ShapeDtypeStruct(enc_bias.shape, f32),
            jax.ShapeDtypeStruct(dec_weight.shape, bf),
        ],
        in_specs=[in_hbm] * 5 + [pl.BlockSpec(memory_space=pltpu.SMEM)],
        out_specs=[in_vmem] * 4,
        scratch_shapes=[
            vmem((TOKENS, D), bf),
            vmem((D, TOKENS), bf),
            vmem((D, BLOCK), bf),
            vmem((LAYERS, BLOCK, D), bf),
            vmem((TILE, D), bf),
            vmem((1, BLOCK), f32),
            vmem((TOKENS, BLOCK), f32),
            vmem((TOKENS, LAYERS * BLOCK), bf),
            vmem((CHIPS, 2, TILE, D), bf),
            vmem((CHIPS, TILE, D), bf),
            vmem((CHUNKS, CHIPS, TILE, CW), bf),
            vmem((CHUNKS, CHIPS, TILE, CW), bf),
            vmem((TOKENS, D), bf),
            vmem((TOKENS, LAYERS * BLOCK), f32),
            vmem((TOKENS, LAYERS * BLOCK), bf),
            vmem((LAYERS, TOKENS, BLOCK), bf),
            vmem((TOKENS, BLOCK), f32),
            vmem((3, BLOCK, D), f32),
            vmem((2, 8, 128), f32),
            vmem((CHIPS, 8, 128), f32),
            vmem((LAYERS, 8, 128), f32),
            dma((5,)),
            dma((CHIPS,)),
            dma((CHIPS,)),
            dma((CHIPS,)),
            dma((CHIPS,)),
            dma((LAYERS, CHIPS)),
            dma((LAYERS, CHIPS)),
            dma((CHIPS,)),
            dma((CHIPS,)),
            dma((CHUNKS, CHIPS)),
            dma((CHUNKS, CHIPS)),
            dma((CHUNKS, CHIPS)),
            dma((CHUNKS, CHIPS)),
            dma((CHUNKS, CHIPS)),
            dma((CHUNKS, CHIPS)),
            dma((LAYERS, len(GROUPS))),
            dma((LAYERS, len(GROUPS))),
            dma((CHIPS + LAYERS - 1,)),
            dma((CHIPS + LAYERS - 1,)),
        ],
        compiler_params=pltpu.CompilerParams(
            collective_id=0, has_side_effects=True, vmem_limit_bytes=47 * 2**20
        ),
        cost_estimate=pl.CostEstimate(
            flops=14 * 2 * TOKENS * D * BLOCK, bytes_accessed=10 * 2**20, transcendentals=0
        ),
        name="transcoder_step",
    )(residual, target, enc_weight, enc_bias, dec_weight, jnp.swapaxes(active, 1, 2))
    return (
        loss[0, 0] * (0.5 / (LAYERS * TOKENS * D)),
        enc_grad * jnp.asarray(1.0 / TILE, bf),
        bias_grad * (1.0 / TILE),
        dec_grad * jnp.asarray(1.0 / TILE, bf),
    )


def shifted(value, axis, steps):
    count = lax.axis_size(axis)
    leading, last = (max(0, -steps), min(count, count - steps))
    return lax.ppermute(value, axis, [(source, source + steps) for source in range(leading, last)])


def slot_list(active, layer, my_block, slot_count):
    block_ids = lax.dynamic_index_in_dim(active, layer, 0, keepdims=False)
    hit = jnp.any(block_ids == my_block, axis=1).astype(jnp.int32)
    every = jnp.arange(NTILE, dtype=jnp.int32)
    place = jnp.cumsum(hit) - 1
    chosen = (hit[None, :] == 1) & (
        place[None, :] == jnp.arange(slot_count, dtype=jnp.int32)[:, None]
    )
    tile_ids = jnp.sum(jnp.where(chosen, every[None, :], 0), axis=1)
    filled = jnp.sum(chosen.astype(jnp.float32), axis=1)
    return (tile_ids, filled)


def shards(residual, target, enc_weight, enc_bias, dec_weight, active):
    layers = dec_weight.shape[0]
    feat_dev = enc_weight.shape[2]
    layer_index = lax.axis_index("layer")
    my_block = lax.axis_index("latent") * feat_dev // BLOCK
    slot_count = CAP
    slot_rows = slot_count * TILE
    full_inputs = lax.all_gather(residual[0], "latent", axis=0, tiled=True).reshape(NTILE, TILE, D)
    own_tiles, own_filled = slot_list(active, layer_index, my_block, slot_count)
    rows = jnp.take(full_inputs, own_tiles, axis=0).reshape(slot_rows, D)
    preact = jnp.dot(rows, enc_weight[0], preferred_element_type=jnp.float32) + enc_bias[0][None, :]
    live = jnp.repeat(own_filled, TILE)[:, None]
    sparse_codes = (jnp.maximum(preact, 0.0) * live).astype(jnp.bfloat16)
    dec_all = dec_weight[:, 0]

    def take_source(carry, portion, source):
        writes, kept = carry
        usable = (source >= 0) & (source <= layer_index)
        source_idx = jnp.clip(source, 0, layers - 1)
        portion = jnp.where(usable, portion, jnp.zeros_like(portion))
        tile_ids, _ = slot_list(active, source_idx, my_block, slot_count)
        weight = lax.dynamic_index_in_dim(dec_all, source_idx, 0, keepdims=False)
        product = jnp.dot(portion, weight, preferred_element_type=jnp.float32).reshape(
            slot_count, TILE, D
        )
        writes = writes.at[tile_ids].add(product)
        kept = jnp.where(usable, kept.at[source_idx].set(portion), kept)
        return (writes, kept)

    start_state = (
        jnp.zeros((NTILE, TILE, D), jnp.float32),
        jnp.zeros((layers, slot_rows, feat_dev), jnp.bfloat16),
    )
    state = take_source(start_state, sparse_codes, layer_index)
    moving = sparse_codes
    for hop in range(1, layers):
        moving = shifted(moving, "layer", 1)
        state = take_source(state, moving, layer_index - hop)
    writes, kept = state
    recon = lax.psum_scatter(
        writes.reshape(NTILE * TILE, D), "latent", scatter_dimension=0, tiled=True
    )
    errors = recon - target[0].astype(jnp.float32)
    total = lax.psum(jnp.sum(errors * errors), ("layer", "latent"))
    loss = 0.5 * total / (layers * NTILE * TILE * D)
    full_errors = lax.all_gather(errors.astype(jnp.bfloat16), "latent", axis=0, tiled=True).reshape(
        NTILE, TILE, D
    )
    dec_grads = []
    code_grads = []
    for source in range(layers):
        tile_ids, _ = slot_list(active, source, my_block, slot_count)
        error_part = jnp.take(full_errors, tile_ids, axis=0).reshape(slot_rows, D)
        grad = lax.dot_general(
            kept[source], error_part, (((0,), (0,)), ((), ())), preferred_element_type=jnp.float32
        )
        dec_grads.append((grad / TILE).astype(jnp.bfloat16))
        back = lax.dot_general(
            error_part,
            dec_all[source],
            (((1,), (1,)), ((), ())),
            preferred_element_type=jnp.float32,
        )
        code_grads.append(jnp.where(source <= layer_index, back, jnp.zeros_like(back)))
    dec_grad = jnp.stack(dec_grads)[:, None]
    code_grad = jnp.stack(code_grads)
    running = code_grad
    for hop in range(1, layers):
        running = code_grad + shifted(running, "layer", -1)
    mine = lax.dynamic_index_in_dim(running, layer_index, 0, keepdims=False)
    pre_grad = jnp.where(preact > 0, mine, jnp.zeros_like(mine)) * live
    bias_grad = (jnp.sum(pre_grad, axis=0) / TILE)[None]
    enc_term = lax.dot_general(
        rows,
        pre_grad.astype(jnp.bfloat16),
        (((0,), (0,)), ((), ())),
        preferred_element_type=jnp.float32,
    )
    enc_grad = (enc_term / TILE).astype(jnp.bfloat16)[None]
    return (loss, enc_grad, bias_grad, dec_grad)


def solution(mesh):
    in_specs = (
        P("layer", "latent", None),
        P("layer", "latent", None),
        P("layer", None, "latent"),
        P("layer", "latent"),
        P(None, "layer", "latent", None),
        P(),
    )
    out_specs = (
        P(),
        P("layer", None, "latent"),
        P("layer", "latent"),
        P(None, "layer", "latent", None),
    )
    one_tile_each = mesh.shape["latent"] == NTILE and mesh.shape["layer"] == LAYERS
    step = fused if one_tile_each else shards
    return jax.shard_map(step, mesh=mesh, in_specs=in_specs, out_specs=out_specs, check_vma=False)
```
